128 devices in a mesh: grp: 4 (over z), dom: 32 (over y, x, core).
Axes of the slice: x: 4, y: 4, z: 4, core: 2. Of those that a mesh axis runs over, the one named last changes fastest.
Arguments:
- features: bfloat16 [32768, 768], P(('grp', 'dom')), may hold values from -6 to 6
- text_embed: bfloat16 [32768, 512], P(('grp', 'dom')), may hold values from -6 to 6
- adjacency: bfloat16 [32768, 1024], P(('grp', 'dom')), may hold values from 0 to 0.0625
- block_cols: int32 [256, 8], P(('grp', 'dom')), may hold values from 0 to 255, as said below
- positive: int32 [32768], P(('grp', 'dom')), may hold values from 0 to 32767
- self_weight: bfloat16 [768, 512], replicated, may hold values from -0.21875 to 0.21875
- nbr_weight: bfloat16 [768, 512], replicated, may hold values from -0.21875 to 0.21875
- hidden_bias: float32 [512], replicated, may hold values from -3 to 3
Outputs:
- embedding: bfloat16 [32768, 512], P(('grp', 'dom'))
- mean_loss: float32 [], replicated
- grad_self: float32 [768, 512], replicated
- grad_nbr: float32 [768, 512], replicated
- grad_bias: float32 [512], replicated
The draws below stay inside these ranges and needn't reach their ends.
Inputs may be any that keep to these rules, and one draw needn't show every extreme that they name: `block_cols`: each listed block of a block row lies on a device of the row's own partition group, or on the device of the same partition index in some group; the last of the K entries is the one that may lie in another group.
All inputs are finite; a program needn't handle non-finite values.
Results may differ from the reference program's by a relative error of at most 0.0118.
Values may be sent and summed in bfloat16 or wider, within the bound.
A program may use at most 192 MiB of HBM per device.

```python
import jax
import jax.numpy as jnp
from jax import lax

D = 768
LATENT_NEURONS = 512
BLOCK = 128
K = 8
RB_DEV = 2
NODES = 32768
ROWBLOCKS = 256
N_GRP = 4
N_DOM = 32


def draw_block_cols(key, part):
    key = jax.random.fold_in(key, 7)
    first_key, random_key_two, third_key, fourth_key = jax.random.split(key, 4)
    row_ids = jnp.arange(ROWBLOCKS, dtype=jnp.int32)[:, None]
    device_ids = row_ids // RB_DEV
    group_ids = device_ids // N_DOM
    domain_ids = device_ids % N_DOM
    local_domain = jax.random.randint(first_key, (ROWBLOCKS, K - 1), 0, N_DOM, dtype=jnp.int32)
    local_within = jax.random.randint(random_key_two, (ROWBLOCKS, K - 1), 0, RB_DEV, dtype=jnp.int32)
    inside = (group_ids * N_DOM + local_domain) * RB_DEV + local_within
    cross_group = jax.random.randint(third_key, (ROWBLOCKS, 1), 0, N_GRP, dtype=jnp.int32)
    cross_within = jax.random.randint(fourth_key, (ROWBLOCKS, 1), 0, RB_DEV, dtype=jnp.int32)
    outside = (cross_group * N_DOM + domain_ids) * RB_DEV + cross_within
    return jnp.concatenate([inside, outside], axis=1).astype(jnp.int32)


def set_ends(entries, key, smallest, top_value):
    index_at = [jax.random.randint(jax.random.fold_in(key, axis), (), 0, length) for axis, length in enumerate(entries.shape)]
    main_axis = entries.shape.index(max(entries.shape))
    beside = index_at[:main_axis] + [(index_at[main_axis] + 1) % entries.shape[main_axis]] + index_at[main_axis + 1:]
    return entries.at[tuple(index_at)].set(smallest).at[tuple(beside)].set(top_value)


def block_scale(key, dims, pieces, low, largest):
    def one(position, blocks):
        steps = jax.random.uniform(jax.random.fold_in(jax.random.fold_in(key, 6), position), (blocks,), jnp.float32, low / len(pieces), largest / len(pieces))
        return jnp.repeat(jnp.exp(steps), dims[position] // blocks).reshape((-1,) + (1,) * (len(dims) - position - 1))

    factor_of = one(*pieces[0])
    for cut in pieces[1:]:
        factor_of = factor_of * one(*cut)
    return factor_of


def scatter_about(stream_key, shape, deviation, most, pieces=(), kind=jnp.bfloat16):
    loudness = block_scale(stream_key, shape, pieces, -0.22, 0.18) if pieces else 1.0
    values = jax.random.normal(stream_key, shape, jnp.float32) * deviation * loudness
    return jnp.minimum(jnp.maximum(values, -most), most).astype(kind)


def setup_inputs(seed: int = 0) -> dict:
    keys = jax.random.split(jax.random.key(seed), 9)
    return {
        "features": scatter_about(keys[0], (NODES, D), 1.0, 6.0, ((0, 128),)),
        "text_embed": scatter_about(keys[1], (NODES, LATENT_NEURONS), 1.0, 6.0, ((0, 128),)),
        "adjacency": jnp.clip(0.0625 * jax.random.uniform(keys[2], (NODES, K * BLOCK), jnp.float32) ** block_scale(keys[2], (NODES, K * BLOCK), ((0, 128),), -0.2, 0.2), 0.0, 0.0625).astype(jnp.bfloat16),
        "block_cols": draw_block_cols(jax.random.fold_in(keys[8], 71), 0),
        "positive": set_ends(jax.random.randint(keys[4], (NODES,), 0, NODES), jax.random.fold_in(keys[4], 1), 0, NODES - 1).astype(jnp.int32),
        "self_weight": scatter_about(keys[5], (D, LATENT_NEURONS), D ** -0.5, 0.21875),
        "nbr_weight": scatter_about(keys[6], (D, LATENT_NEURONS), D ** -0.5, 0.21875),
        "hidden_bias": scatter_about(keys[7], (LATENT_NEURONS,), 0.5, 3.0, (), jnp.float32),
    }


epsilon = 1e-05
inverse_softmax_coldness = 10.0
highest = lax.Precision.HIGHEST

def rms_scale(values):
    return lax.rsqrt(lax.optimization_barrier(jnp.mean(values * values, axis=1, keepdims=True)) + epsilon)

def reference(features, text_embed, adjacency, block_cols, positive, self_weight, nbr_weight, hidden_bias):
    attribute_tiles = features.reshape(ROWBLOCKS, BLOCK, D)
    adj_rows = adjacency.reshape(ROWBLOCKS, BLOCK, K * BLOCK)

    def aggregate(operands):
        adj_block, column_ids = operands
        chosen = attribute_tiles[column_ids].reshape(K * BLOCK, D)
        return jnp.dot(adj_block, chosen, preferred_element_type=jnp.float32)
    aggregated = lax.map(aggregate, (adj_rows, block_cols)).reshape(NODES, D)
    self_term = jnp.dot(features, self_weight, preferred_element_type=jnp.float32)
    nbr_term = jnp.dot(aggregated, nbr_weight.astype(jnp.float32), precision=highest)
    pre_act = self_term + nbr_term + hidden_bias
    hidden = jnp.maximum(pre_act, 0.0)
    scale_rows = rms_scale(hidden)
    normed = hidden * scale_rows
    half_unit_vector = normed.astype(jnp.bfloat16)
    text_wide = text_embed.astype(jnp.float32)
    text_unit = (text_wide * rms_scale(text_wide)).astype(jnp.bfloat16)
    normalizing_multiplier = inverse_softmax_coldness / LATENT_NEURONS

    def contrast(operands):
        queries, matching_labels = operands
        similarity_logits = jnp.dot(queries, text_unit.T, preferred_element_type=jnp.float32) * normalizing_multiplier
        exponent = jnp.exp(similarity_logits)
        totals = lax.optimization_barrier(jnp.sum(exponent, axis=1))
        weighted = jnp.dot(exponent.astype(jnp.bfloat16), text_unit, preferred_element_type=jnp.float32)
        picked = text_unit[matching_labels].astype(jnp.float32)
        return (totals, weighted, picked)
    totals, weighted, picked = lax.map(contrast, (half_unit_vector.reshape(ROWBLOCKS, BLOCK, LATENT_NEURONS), positive.reshape(ROWBLOCKS, BLOCK)))
    totals = totals.reshape(NODES)
    weighted = weighted.reshape(NODES, LATENT_NEURONS)
    picked = picked.reshape(NODES, LATENT_NEURONS)
    pos_logit = lax.optimization_barrier(jnp.sum(half_unit_vector.astype(jnp.float32) * picked, axis=1)) * normalizing_multiplier
    mean_loss = jnp.sum(jnp.log(totals) - pos_logit) / NODES
    grad_unit = normalizing_multiplier * (weighted / totals[:, None] - picked)
    grad_hidden = scale_rows * (grad_unit - normed * lax.optimization_barrier(jnp.mean(grad_unit * normed, axis=1, keepdims=True)))
    grad_pre = jnp.where(pre_act > 0, grad_hidden, 0.0)
    grad_self = jnp.dot(features.astype(jnp.float32).T, grad_pre, precision=highest)
    grad_nbr = jnp.dot(aggregated.T, grad_pre, precision=highest)
    grad_bias = lax.optimization_barrier(jnp.sum(grad_pre, axis=0))
    return (hidden.astype(jnp.bfloat16), mean_loss, grad_self, grad_nbr, grad_bias)
```

```python
import functools

import jax
import jax.numpy as jnp
from jax import lax
from jax.experimental import pallas as pl
from jax.experimental.pallas import tpu as pltpu
from jax.sharding import PartitionSpec as P

MESH = pl.DeviceIdType.MESH
D = 768
H = 512
BLOCK = 128
K = 8
ROWS = 256
HALF = 128
N_GRP = 4
N_DOM = 32
NODES = 32768
SLAB = N_DOM * ROWS
CHUNK = 1024

EPS = 1e-05
SCALE = 10.0 / H
LOG2E = 1.4426950408889634

BF = jnp.bfloat16
F32 = jnp.float32

STEPS = (0, -1, 1, 2)
GATHER_SEMS = 36


def rms_scale(values):
    return lax.rsqrt(jnp.mean(values * values, axis=1, keepdims=True) + EPS)


def dot(a, b):
    return jnp.dot(a, b, preferred_element_type=F32)


def dot_nt(a, b):
    return lax.dot_general(a, b, (((1,), (1,)), ((), ())), preferred_element_type=F32)


def dot_tn(a, b):
    return lax.dot_general(a, b, (((0,), (0,)), ((), ())), preferred_element_type=F32)


def kernel(
    feat, text, adj, cols, pos, self_w, nbr_w, bias,
    emb, grads, extra_out,
    F, T, Q, POS, AGG, HID, G, WACC, TACC, WP_S, WP_R, TOT_S, TOT_R,
    SA, RA, SB, RB, SC, RC, EX,
    fs, fr, ts, tr, zs, zr, ms, mr, gs, gr,
):
    g = lax.axis_index("grp")
    d = lax.axis_index("dom")
    c = d % 2
    x = (d // 2) % 4
    y = d // 8

    def dom_at(i, j, cc):
        ux, uy = 1 - cc, cc
        ax = (x + i * ux + j * uy + 4) % 4
        ay = (y + i * uy + j * ux + 4) % 4
        return (ay * 4 + ax) * 2 + cc

    def prim(k):
        return (g, dom_at(k, 0, c))

    def sec(k):
        return (g, dom_at(0, k, c))

    def zed(k):
        return ((g + k) % 4, d)

    sib = (g, d + 1 - 2 * c)
    pi = x * (1 - c) + y * c
    si = x * c + y * (1 - c)

    def rcopy(src, dst, ssem, rsem, dev):
        return pltpu.make_async_remote_copy(
            src_ref=src, dst_ref=dst, send_sem=ssem, recv_sem=rsem,
            device_id=dev, device_id_type=MESH,
        )

    pending = []

    def send(src, dst, ssem, rsem, dev):
        cp = rcopy(src, dst, ssem, rsem, dev)
        cp.start()
        pending.append(cp)

    def landed(region, ssem, rsem):
        rcopy(region, region, ssem, rsem, sib).wait_recv()

    barrier = pltpu.get_barrier_semaphore()
    partners = [sib] + [f(k) for f in (prim, sec, zed) for k in (1, 2, 3)]
    for dev in partners:
        pl.semaphore_signal(barrier, inc=1, device_id=dev, device_id_type=MESH)

    own = pl.ds(d * ROWS, ROWS)
    F[own, :] = feat[...]
    tw = text[...].astype(F32)
    T[own, :] = (tw * rms_scale(tw)).astype(BF)
    POS[g] = pos[...]
    pl.semaphore_wait(barrier, len(partners))

    class Gather:
        def __init__(self, tab, ssem, rsem):
            self.tab, self.ss, self.rs = tab, ssem, rsem

        def shard(self, i, j, cc, half=None):
            base = dom_at(i, j, cc) * ROWS
            if half is None:
                return self.tab.at[pl.ds(base, ROWS)]
            return self.tab.at[pl.ds(base + half * HALF, HALF)]

        def send(self, i, j, half, k, dev):
            ref = self.shard(i, j, c, half)
            send(ref, ref, self.ss.at[k], self.rs.at[k], dev)

        def wait(self, i, j, half, k, cc=None):
            ref = self.shard(i, j, c if cc is None else cc, half)
            landed(ref, self.ss.at[k], self.rs.at[k])

        def across(self, a, b):
            self.send(STEPS[a], STEPS[b], None, 20 + 4 * a + b, sib)

        def along(self, a):
            self.send(STEPS[a], 0, None, 4 + 4 * a, sec(1))
            self.send(STEPS[a], 0, None, 5 + 4 * a, sec(-1))

        def first(self):
            self.send(0, 0, None, 0, prim(1))
            self.send(0, 0, None, 1, prim(-1))
            self.along(0)
            self.across(0, 0)

        def second(self):
            self.wait(-1, 0, None, 0)
            self.send(-1, 0, 0, 2, prim(1))
            self.along(1)
            self.across(1, 0)
            self.wait(1, 0, None, 1)
            self.send(1, 0, 1, 3, prim(-1))
            self.along(2)
            self.across(2, 0)

        def turn(self, a):
            self.wait(STEPS[a], -1, None, 4 + 4 * a)
            self.send(STEPS[a], -1, 0, 6 + 4 * a, sec(1))
            self.across(a, 1)
            self.wait(STEPS[a], 1, None, 5 + 4 * a)
            self.send(STEPS[a], 1, 1, 7 + 4 * a, sec(-1))
            self.across(a, 2)

        def third(self):
            self.wait(2, 0, 0, 2)
            self.wait(2, 0, 1, 3)
            self.along(3)
            self.across(3, 0)

        def end(self, a):
            self.wait(STEPS[a], 2, 0, 6 + 4 * a)
            self.wait(STEPS[a], 2, 1, 7 + 4 * a)
            self.across(a, 3)

        def sibling(self):
            for a in range(4):
                for b in range(4):
                    self.wait(STEPS[a], STEPS[b], None, 20 + 4 * a + b, 1 - c)

    gf = Gather(F, fs, fr)
    gt = Gather(T, ts, tr)

    gf.first()
    for k in (1, 2, 3):
        mine = F.at[pl.ds(SLAB + g * ROWS, ROWS)]
        send(feat, mine, zs.at[k - 1], zr.at[k - 1], zed(k))
        send(pos, POS.at[g], zs.at[k + 2], zr.at[k + 2], zed(k))
    gf.second()
    gf.turn(0)
    gf.third()
    gf.turn(1)
    gf.turn(2)
    gf.turn(3)
    gt.first()
    for a in range(4):
        gf.end(a)
    gt.second()
    gf.sibling()

    def from_zed(k):
        return (g - k + 4) % 4

    for k in (1, 2, 3):
        o = from_zed(k)
        landed(F.at[pl.ds(SLAB + o * ROWS, ROWS)], zs.at[k - 1], zr.at[k - 1])

    for r in range(2):
        rows = pl.ds(r * BLOCK, BLOCK)
        agg = jnp.zeros((BLOCK, D), F32)
        for k in range(K):
            b = cols[r, k]
            device = b // 2
            group, domain = device // N_DOM, device % N_DOM
            at = jnp.where(group == g, domain * 2 + b % 2, SLAB // BLOCK + group * 2 + b % 2)
            agg = agg + dot(adj[rows, k * BLOCK:(k + 1) * BLOCK], F[pl.ds(at * BLOCK, BLOCK), :])
        high = agg.astype(BF)
        low = (agg - high.astype(F32)).astype(BF)
        AGG[pl.ds(c * ROWS + r * BLOCK, BLOCK), :] = high
        pre = (
            dot(feat[rows, :], self_w[...])
            + (dot(high, nbr_w[...]) + dot(low, nbr_w[...]))
            + bias[...]
        )
        hidden = jnp.maximum(pre, 0.0)
        HID[rows, :] = hidden
        emb[rows, :] = hidden.astype(BF)
        Q[g, rows, :] = (hidden * rms_scale(hidden)).astype(BF)

    for k in (1, 2, 3):
        send(Q.at[g], Q.at[g], zs.at[k + 5], zr.at[k + 5], zed(k))
    agg_own = AGG.at[pl.ds(c * ROWS, ROWS)]
    send(agg_own, agg_own, ms.at[0], mr.at[0], sib)

    gt.turn(0)
    gt.third()
    for a in (1, 2, 3):
        gt.turn(a)
    for a in range(4):
        gt.end(a)
    gt.sibling()
    for k in (1, 2, 3):
        o = from_zed(k)
        landed(POS.at[o], zs.at[k + 2], zr.at[k + 2])

    lanes = lax.broadcasted_iota(jnp.int32, (ROWS, CHUNK), 1)

    for k in (1, 2, 3, 0):
        o = (g + k) % 4
        if k:
            landed(Q.at[o], zs.at[9 - k], zr.at[9 - k])
        WACC[...] = jnp.zeros_like(WACC)
        TACC[...] = jnp.zeros_like(TACC)

        @pl.loop(0, SLAB // CHUNK)
        def _(n, o=o):
            part = T[pl.ds(n * CHUNK, CHUNK), :]
            e = jnp.exp2(dot_nt(Q[o], part) * (SCALE * LOG2E))
            tot = TACC[...]
            for m in range(CHUNK // 128):
                tot = tot + e[:, m * 128:(m + 1) * 128]
            TACC[...] = tot
            where = POS[o] - (g * SLAB + n * CHUNK)
            hot = jnp.concatenate([where] * (CHUNK // 128), axis=1) == lanes
            hot = hot.astype(F32).astype(BF)
            WACC[...] += dot(jnp.concatenate([e.astype(BF), hot], axis=0), part)

        if k:
            WP_S[k - 1] = WACC[...].astype(BF)
            TOT_S[k - 1] = TACC[...]
            send(WP_S.at[k - 1], WP_R.at[k - 1], zs.at[k + 8], zr.at[k + 8], zed(k))
            send(TOT_S.at[k - 1], TOT_R.at[k - 1], zs.at[k + 11], zr.at[k + 11], zed(k))

    for k in (1, 2, 3):
        landed(WP_R.at[k - 1], zs.at[k + 8], zr.at[k + 8])
        landed(TOT_R.at[k - 1], zs.at[k + 11], zr.at[k + 11])

    weighted = WACC[0:ROWS, :]
    picked = WACC[ROWS:2 * ROWS, :]
    lanes_total = TACC[...]
    for k in range(3):
        weighted = weighted + WP_R[k, 0:ROWS, :].astype(F32)
        picked = picked + WP_R[k, ROWS:2 * ROWS, :].astype(F32)
        lanes_total = lanes_total + TOT_R[k]
    totals = jnp.sum(lanes_total, axis=1, keepdims=True)
    pos_logit = jnp.sum(Q[g].astype(F32) * picked, axis=1, keepdims=True) * SCALE
    loss = jnp.sum(jnp.log(totals) - pos_logit, axis=0, keepdims=True)
    hidden = HID[...]
    scale_rows = rms_scale(hidden)
    normed = hidden * scale_rows
    unit = SCALE * (weighted / totals - picked)
    back = scale_rows * (unit - normed * jnp.mean(unit * normed, axis=1, keepdims=True))
    grad_pre = jnp.where(hidden > 0, back, 0.0)
    G[pl.ds(c * ROWS, ROWS), :] = grad_pre.astype(BF)
    g_own = G.at[pl.ds(c * ROWS, ROWS)]
    send(g_own, g_own, ms.at[1], mr.at[1], sib)

    bias_sum = jnp.sum(grad_pre, axis=0, keepdims=True)
    parts = [bias_sum[:, m * 128:(m + 1) * 128] for m in range(4)]
    parts.append(jnp.broadcast_to(loss, (1, 128)))
    parts.append(jnp.zeros((3, 128), F32))
    value = jnp.concatenate(parts, axis=0)

    def split(v):
        high = v.astype(BF).astype(F32)
        return jnp.concatenate([high, v - high], axis=0).astype(BF)

    def join(pair):
        return pair[0:8, :] + pair[8:16, :]

    sib_rows = pl.ds((1 - c) * ROWS, ROWS)
    landed(AGG.at[sib_rows], ms.at[0], mr.at[0])
    landed(G.at[sib_rows], ms.at[1], mr.at[1])
    pair = F[pl.ds((d // 2) * 2 * ROWS, 2 * ROWS), :]
    left = jnp.where(c == 0, pair, AGG[...])
    extra = split(value)
    for m in range(4):
        SA[m, 0:D, :] = dot_tn(left, G[:, m * 128:(m + 1) * 128]).astype(BF)
        SA[m, D:D + 16, :] = extra

    def exchange(S, R, at, ring, base, rows):
        for k in (1, 2, 3):
            send(S.at[(at + k) % 4], R.at[k - 1], gs.at[base + k], gr.at[base + k], ring(k))
        for k in (1, 2, 3):
            landed(R.at[k - 1], gs.at[base + k], gr.at[base + k])
        total = S[at].astype(F32)
        for k in range(3):
            total = total + R[k].astype(F32)
        return total[0:rows, :], join(total[rows:rows + 16, :])

    total, value = exchange(SA, RA, pi, prim, 0, D)
    extra = split(value)
    for m in range(4):
        SB[m, 0:192, :] = total[m * 192:(m + 1) * 192, :].astype(BF)
        SB[m, 192:208, :] = extra
    total, value = exchange(SB, RB, si, sec, 3, 192)
    extra = split(value)
    for m in range(4):
        SC[m, 0:48, :] = total[m * 48:(m + 1) * 48, :].astype(BF)
        SC[m, 48:64, :] = extra
    total, value = exchange(SC, RC, g, zed, 6, 48)

    EX[c] = split(value)
    send(EX.at[c], EX.at[c], ms.at[2], mr.at[2], sib)

    def spread(ring, base, row_of, rows):
        ref = grads.at[c, pl.ds(row_of(0), rows)]
        for k in (1, 2, 3):
            send(ref, ref, gs.at[base + k], gr.at[base + k], ring(k))
        for k in (1, 2, 3):
            landed(grads.at[c, pl.ds(row_of(-k), rows)], gs.at[base + k], gr.at[base + k])

    def at(p, s, z):
        return ((pi + p + 4) % 4) * 768 + ((si + s + 4) % 4) * 192 + ((g + z + 4) % 4) * 48

    grads[c, pl.ds(at(0, 0, 0), 48), :] = total.astype(BF)
    spread(zed, 9, lambda k: at(0, 0, k), 48)
    spread(sec, 12, lambda k: pi * 768 + ((si + k + 4) % 4) * 192, 192)

    def block(k, cc=None):
        which = c if cc is None else cc
        index = x * (1 - which) + y * which
        return grads.at[which, pl.ds(((index + k + 4) % 4) * 768, 768)]

    for k in (1, 2, 3):
        send(block(0), block(0), gs.at[15 + k], gr.at[15 + k], prim(k))
    send(block(0), block(0), ms.at[3], mr.at[3], sib)
    for k in (1, 2, 3):
        landed(block(-k), gs.at[15 + k], gr.at[15 + k])
        send(block(-k), block(-k), ms.at[3 + k], mr.at[3 + k], sib)
    landed(EX.at[1 - c], ms.at[2], mr.at[2])
    extra_out[...] = join(EX[0].astype(F32)) + join(EX[1].astype(F32))
    for k in range(4):
        landed(block(-k, 1 - c), ms.at[3 + k], mr.at[3 + k])
    for cp in pending:
        cp.wait_send()


def shards(features, text_embed, adjacency, block_cols, positive, self_weight, nbr_weight, hidden_bias):
    pos = jnp.broadcast_to(positive[:, None], (ROWS, 128))
    vmem = pl.BlockSpec(memory_space=pltpu.VMEM)
    smem = pl.BlockSpec(memory_space=pltpu.SMEM)
    dma = pltpu.SemaphoreType.DMA
    emb, grads, extra = pl.pallas_call(
        kernel,
        name="step",
        out_shape=(
            jax.ShapeDtypeStruct((ROWS, H), BF),
            jax.ShapeDtypeStruct((2, 4 * D, 128), BF),
            jax.ShapeDtypeStruct((8, 128), F32),
        ),
        in_specs=[vmem, vmem, vmem, smem, vmem, vmem, vmem, vmem],
        out_specs=(vmem, vmem, vmem),
        scratch_shapes=[
            pltpu.VMEM((SLAB + N_GRP * ROWS, D), BF),
            pltpu.VMEM((SLAB, H), BF),
            pltpu.VMEM((N_GRP, ROWS, H), BF),
            pltpu.VMEM((N_GRP, ROWS, 128), jnp.int32),
            pltpu.VMEM((2 * ROWS, D), BF),
            pltpu.VMEM((ROWS, H), F32),
            pltpu.VMEM((2 * ROWS, H), BF),
            pltpu.VMEM((2 * ROWS, H), F32),
            pltpu.VMEM((ROWS, 128), F32),
            pltpu.VMEM((3, 2 * ROWS, H), BF),
            pltpu.VMEM((3, 2 * ROWS, H), BF),
            pltpu.VMEM((3, ROWS, 128), F32),
            pltpu.VMEM((3, ROWS, 128), F32),
            pltpu.VMEM((4, D + 16, 128), BF),
            pltpu.VMEM((3, D + 16, 128), BF),
            pltpu.VMEM((4, 208, 128), BF),
            pltpu.VMEM((3, 208, 128), BF),
            pltpu.VMEM((4, 64, 128), BF),
            pltpu.VMEM((3, 64, 128), BF),
            pltpu.VMEM((2, 16, 128), BF),
            dma((GATHER_SEMS,)), dma((GATHER_SEMS,)),
            dma((GATHER_SEMS,)), dma((GATHER_SEMS,)),
            dma((15,)), dma((15,)),
            dma((7,)), dma((7,)),
            dma((19,)), dma((19,)),
        ],
        compiler_params=pltpu.CompilerParams(
            collective_id=0, has_side_effects=True, vmem_limit_bytes=56 * 2**20
        ),
        cost_estimate=pl.CostEstimate(
            flops=30 * 10**9, bytes_accessed=8 * 2**20, transcendentals=8 * 2**20
        ),
    )(
        features, text_embed, adjacency, block_cols, pos, self_weight, nbr_weight,
        hidden_bias.reshape(1, H),
    )
    wide = grads.reshape(2, 4, D, 128).transpose(0, 2, 1, 3).reshape(2, D, H).astype(F32)
    return emb, extra[4, 0] / NODES, wide[0], wide[1], extra[0:4].reshape(H)


def solution(mesh):
    rows = P(("grp", "dom"), None)
    return jax.shard_map(
        shards,
        mesh=mesh,
        in_specs=(rows, rows, rows, rows, P(("grp", "dom")), P(), P(), P()),
        out_specs=(rows, P(), P(), P(), P()),
        check_vma=False,
    )
```

```python
import functools

import jax
import jax.numpy as jnp
from jax import lax
from jax.experimental import pallas as pl
from jax.experimental.pallas import tpu as pltpu
from jax.sharding import PartitionSpec as P

MESH = pl.DeviceIdType.MESH
D = 768
H = 512
BLOCK = 128
K = 8
ROWS = 256
HALF = 128
N_GRP = 4
N_DOM = 32
NODES = 32768
SLAB = N_DOM * ROWS
CHUNK = 2048

EPS = 1e-05
SCALE = 10.0 / H
LOG2E = 1.4426950408889634

BF = jnp.bfloat16
F32 = jnp.float32

ORDER = (
    (-1, 0, 0), (1, 0, 1), (-1, 0, 1), (1, 0, 0), (0, -1, 0), (0, 1, 0), (0, -1, 1), (0, 1, 1),
    (2, 0, 0), (-1, 1, 0), (-1, -1, 0), (2, 0, 1), (1, -1, 1), (1, 1, 1), (-1, -1, 1), (-1, 1, 1),
    (1, -1, 0), (1, 1, 0), (0, 2, 0), (0, 2, 1), (2, -1, 0), (2, 1, 0), (-1, 2, 0), (2, 1, 1),
    (2, -1, 1), (1, 2, 1), (-1, 2, 1), (1, 2, 0), (2, 2, 0), (2, 2, 1),
)
SHARDS = (
    (0, 0), (-1, 0), (1, 0), (0, -1), (0, 1), (2, 0), (-1, -1), (-1, 1),
    (1, -1), (1, 1), (0, 2), (2, -1), (2, 1), (-1, 2), (1, 2), (2, 2),
)
UNITS = (7, 15, 24, 29)
GATHER_SEMS = len(ORDER) + len(SHARDS)


def rms_scale(values):
    return lax.rsqrt(jnp.mean(values * values, axis=1, keepdims=True) + EPS)


def dot(a, b):
    return jnp.dot(a, b, preferred_element_type=F32)


def dot_nt(a, b):
    return lax.dot_general(a, b, (((1,), (1,)), ((), ())), preferred_element_type=F32)


def column(row):
    return jnp.transpose(jnp.broadcast_to(row, (128, ROWS)))


def kernel(
    feat, text, adj_h, cols, pos, self_h, nbr_h, bias,
    emb, grads, extra_out,
    F, T, Q, POS, PCOL, AGG, HID, G, LT, W_OWN, T_OWN, WACC, TACC, PACC, W_S, W_R, P_R, TOT_S, TOT_R,
    SA, RA, SB, RB, SC, RC, EX, adj, self_w, nbr_w,
    fs, fr, ts, tr, zs, zr, ms, mr, gs, gr, ls,
):
    g = lax.axis_index("grp")
    d = lax.axis_index("dom")
    c = d % 2
    x = (d // 2) % 4
    y = d // 8
    loads = [
        pltpu.make_async_copy(src, dst, ls.at[n])
        for n, (src, dst) in enumerate(((adj_h, adj), (self_h, self_w), (nbr_h, nbr_w)))
    ]
    for load in loads:
        load.start()

    def dom_at(i, j, cc):
        ux, uy = 1 - cc, cc
        ax = (x + i * ux + j * uy + 4) % 4
        ay = (y + i * uy + j * ux + 4) % 4
        return (ay * 4 + ax) * 2 + cc

    def prim(k):
        return (g, dom_at(k, 0, c))

    def sec(k):
        return (g, dom_at(0, k, c))

    def zed(k):
        return ((g + k) % 4, d)

    sib = (g, d + 1 - 2 * c)
    pi = x * (1 - c) + y * c
    si = x * c + y * (1 - c)

    def rcopy(src, dst, ssem, rsem, dev):
        return pltpu.make_async_remote_copy(
            src_ref=src, dst_ref=dst, send_sem=ssem, recv_sem=rsem,
            device_id=dev, device_id_type=MESH,
        )

    pending = []

    def send(src, dst, ssem, rsem, dev):
        cp = rcopy(src, dst, ssem, rsem, dev)
        cp.start()
        pending.append(cp)

    def landed(region, ssem, rsem):
        rcopy(region, region, ssem, rsem, sib).wait_recv()

    barrier = pltpu.get_barrier_semaphore()
    partners = [sib] + [f(k) for f in (prim, sec, zed) for k in (1, 2, 3)]
    for dev in partners:
        pl.semaphore_signal(barrier, inc=1, device_id=dev, device_id_type=MESH)

    own = pl.ds(d * ROWS, ROWS)
    F[own, :] = feat[...]
    tw = text[...].astype(F32)
    T[own, :] = (tw * rms_scale(tw)).astype(BF)
    POS[g] = jnp.broadcast_to(pos[...].astype(F32), (8, ROWS))
    pl.semaphore_wait(barrier, len(partners))

    class Gather:
        def __init__(self, tab, ssem, rsem):
            self.tab, self.ss, self.rs = tab, ssem, rsem

        def shard(self, i, j, cc, half=None):
            base = dom_at(i, j, cc) * ROWS
            if half is None:
                return self.tab.at[pl.ds(base, ROWS)]
            return self.tab.at[pl.ds(base + half * HALF, HALF)]

        def send(self, key, to, dev):
            ref = self.shard(key[0], key[1], c, key[2])
            k = ORDER.index(to + (key[2],))
            send(ref, ref, self.ss.at[k], self.rs.at[k], dev)

        def across(self, i, j):
            ref = self.shard(i, j, c)
            k = len(ORDER) + SHARDS.index((i, j))
            send(ref, ref, self.ss.at[k], self.rs.at[k], sib)

        def along(self, i, h):
            self.send((i, 0, h), (i, -1), sec(1))
            self.send((i, 0, h), (i, 1), sec(-1))

        def start(self):
            self.send((0, 0, 0), (-1, 0), prim(1))
            self.send((0, 0, 1), (1, 0), prim(-1))
            self.send((0, 0, 1), (-1, 0), prim(1))
            self.send((0, 0, 0), (1, 0), prim(-1))
            self.along(0, 0)
            self.along(0, 1)
            self.across(0, 0)
            self.here = set()

        def step(self, n):
            i, j, h = key = ORDER[n]
            landed(self.shard(i, j, c, h), self.ss.at[n], self.rs.at[n])
            if key == (-1, 0, 0):
                self.send(key, (2, 0), prim(1))
            if key == (1, 0, 1):
                self.send(key, (2, 0), prim(-1))
            if j == 0:
                self.along(i, h)
            if j == -1 and h == 0:
                self.send(key, (i, 2), sec(1))
            if j == 1 and h == 1:
                self.send(key, (i, 2), sec(-1))
            if (i, j) in self.here:
                self.across(i, j)
            self.here.add((i, j))

        def sibling(self, i, j):
            k = len(ORDER) + SHARDS.index((i, j))
            landed(self.shard(i, j, 1 - c), self.ss.at[k], self.rs.at[k])

    gf = Gather(F, fs, fr)
    gt = Gather(T, ts, tr)

    gf.start()
    for k in (1, 2, 3):
        mine = F.at[pl.ds(SLAB + g * ROWS, ROWS)]
        send(feat, mine, zs.at[k - 1], zr.at[k - 1], zed(k))
        send(POS.at[g], POS.at[g], zs.at[k + 2], zr.at[k + 2], zed(k))
    for n in range(25):
        gf.step(n)
    gt.start()
    for n in range(25, 30):
        gf.step(n)
    for n in range(2):
        gt.step(n)
    for i, j in SHARDS:
        gf.sibling(i, j)

    def from_zed(k):
        return (g - k + 4) % 4

    for k in (1, 2, 3):
        o = from_zed(k)
        landed(F.at[pl.ds(SLAB + o * ROWS, ROWS)], zs.at[k - 1], zr.at[k - 1])

    for load in loads:
        load.wait()
    for r in range(2):
        rows = pl.ds(r * BLOCK, BLOCK)
        agg = jnp.zeros((BLOCK, D), F32)
        for k in range(K):
            b = cols[r, k]
            device = b // 2
            group, domain = device // N_DOM, device % N_DOM
            at = jnp.where(group == g, domain * 2 + b % 2, SLAB // BLOCK + group * 2 + b % 2)
            agg = agg + dot(adj[rows, k * BLOCK:(k + 1) * BLOCK], F[pl.ds(at * BLOCK, BLOCK), :])
        high = agg.astype(BF)
        low = (agg - high.astype(F32)).astype(BF)
        AGG[pl.ds(c * ROWS + r * BLOCK, BLOCK), :] = high
        pre = (
            dot(feat[rows, :], self_w[...])
            + (dot(high, nbr_w[...]) + dot(low, nbr_w[...]))
            + bias[...]
        )
        hidden = jnp.maximum(pre, 0.0)
        HID[rows, :] = hidden
        emb[rows, :] = hidden.astype(BF)
        Q[g, rows, :] = (hidden * rms_scale(hidden)).astype(BF)

    for k in (1, 2, 3):
        send(Q.at[g], Q.at[g], zs.at[k + 5], zr.at[k + 5], zed(k))
    agg_own = AGG.at[pl.ds(c * ROWS, ROWS)]
    send(agg_own, agg_own, ms.at[0], mr.at[0], sib)

    for k in (1, 2, 3):
        o = from_zed(k)
        landed(POS.at[o], zs.at[k + 2], zr.at[k + 2])
    for o in range(N_GRP):
        PCOL[o * ROWS:(o + 1) * ROWS, :] = column(POS[o, 0:1, :])
    PACC[...] = jnp.zeros_like(PACC)
    lanes = lax.broadcasted_iota(jnp.int32, (N_GRP * ROWS, 128), 1).astype(F32)

    def contrast(o, part, WACC, TACC):
        e = jnp.exp2(dot_nt(Q[o], part) * (SCALE * LOG2E))
        tot = TACC[...]
        for m in range(part.shape[0] // 128):
            tot = tot + e[:, m * 128:(m + 1) * 128]
        TACC[...] = tot
        WACC[...] += dot(e.astype(BF), part)

    def clear(WACC, TACC):
        WACC[...] = jnp.zeros_like(WACC)
        TACC[...] = jnp.zeros_like(TACC)

    def pick(doms, part):
        hot = []
        for dom in doms:
            for m in range(ROWS // 128):
                at = (g * SLAB + dom * ROWS + m * 128).astype(F32)
                hot.append(jnp.where(PCOL[...] - at == lanes, 1.0, 0.0).astype(BF))
        PACC[...] += dot(jnp.concatenate(hot, axis=1), part).astype(BF)

    def gathered(doms):
        return jnp.concatenate([T[pl.ds(dom * ROWS, ROWS), :] for dom in doms], axis=0)

    clear(W_OWN, T_OWN)
    sib_rows = pl.ds((1 - c) * ROWS, ROWS)
    landed(AGG.at[sib_rows], ms.at[0], mr.at[0])
    pair = F[pl.ds((d // 2) * 2 * ROWS, 2 * ROWS), :]
    LT[...] = jnp.transpose(jnp.where(c == 0, pair, AGG[...]))
    done = 2
    for u, last in enumerate(UNITS):
        while done <= last:
            gt.step(done)
            done += 1
        group = SHARDS[4 * u:4 * u + 4]
        for cc in (c, 1 - c):
            if cc is not c:
                for i, j in group:
                    gt.sibling(i, j)
            doms = [dom_at(i, j, cc) for i, j in group]
            part = gathered(doms)
            pick(doms, part)
            contrast(g, part, W_OWN, T_OWN)

    for k in (1, 2, 3):
        o = (g + k) % 4
        ref = PACC.at[pl.ds(o * ROWS, ROWS)]
        send(ref, P_R.at[k - 1], zs.at[k + 8], zr.at[k + 8], zed(k))
    for k in (1, 2, 3):
        o = (g + k) % 4
        landed(Q.at[o], zs.at[9 - k], zr.at[9 - k])
        clear(WACC, TACC)

        @pl.loop(0, SLAB // CHUNK)
        def _(n, o=o):
            contrast(o, T[pl.ds(n * CHUNK, CHUNK), :], WACC, TACC)

        W_S[k - 1] = WACC[...].astype(BF)
        TOT_S[k - 1] = lax.dot_general(
            jnp.ones((8, 128), F32), TACC[...], (((1,), (1,)), ((), ())),
            precision=lax.Precision.HIGHEST, preferred_element_type=F32,
        )
        send(W_S.at[k - 1], W_R.at[k - 1], zs.at[k + 11], zr.at[k + 11], zed(k))
        send(TOT_S.at[k - 1], TOT_R.at[k - 1], zs.at[k + 14], zr.at[k + 14], zed(k))
    for k in (1, 2, 3):
        landed(P_R.at[k - 1], zs.at[k + 8], zr.at[k + 8])
        landed(W_R.at[k - 1], zs.at[k + 11], zr.at[k + 11])
        landed(TOT_R.at[k - 1], zs.at[k + 14], zr.at[k + 14])

    weighted = W_OWN[...]
    picked = PACC[pl.ds(g * ROWS, ROWS), :].astype(F32)
    for k in range(3):
        weighted = weighted + W_R[k].astype(F32)
        picked = picked + P_R[k].astype(F32)
    totals = jnp.sum(T_OWN[...], axis=1, keepdims=True)
    totals = totals + column((TOT_R[0] + TOT_R[1] + TOT_R[2])[0:1, :])[:, 0:1]
    pos_logit = jnp.sum(Q[g].astype(F32) * picked, axis=1, keepdims=True) * SCALE
    loss = jnp.sum(jnp.log(totals) - pos_logit, axis=0, keepdims=True)
    hidden = HID[...]
    scale_rows = rms_scale(hidden)
    normed = hidden * scale_rows
    unit = SCALE * (weighted / totals - picked)
    back = scale_rows * (unit - normed * jnp.mean(unit * normed, axis=1, keepdims=True))
    grad_pre = jnp.where(hidden > 0, back, 0.0)
    G[pl.ds(c * ROWS, ROWS), :] = grad_pre.astype(BF)
    g_own = G.at[pl.ds(c * ROWS, ROWS)]
    send(g_own, g_own, ms.at[1], mr.at[1], sib)

    bias_sum = jnp.sum(grad_pre, axis=0, keepdims=True)
    parts = [bias_sum[:, m * 128:(m + 1) * 128] for m in range(4)]
    parts.append(jnp.broadcast_to(loss, (1, 128)))
    parts.append(jnp.zeros((3, 128), F32))
    value = jnp.concatenate(parts, axis=0)

    def split(v):
        high = v.astype(BF).astype(F32)
        return jnp.concatenate([high, v - high], axis=0).astype(BF)

    def join(pair):
        return pair[0:8, :] + pair[8:16, :]

    landed(G.at[sib_rows], ms.at[1], mr.at[1])
    extra = split(value)
    grad = dot(LT[...], G[...]).astype(BF)
    for m in range(4):
        SA[m, 0:D, :] = grad[:, m * 128:(m + 1) * 128]
        SA[m, D:D + 16, :] = extra

    def exchange(S, R, at, ring, base, rows):
        for k in (1, 2, 3):
            send(S.at[(at + k) % 4], R.at[k - 1], gs.at[base + k], gr.at[base + k], ring(k))
        for k in (1, 2, 3):
            landed(R.at[k - 1], gs.at[base + k], gr.at[base + k])
        total = S[at].astype(F32)
        for k in range(3):
            total = total + R[k].astype(F32)
        return total[0:rows, :], join(total[rows:rows + 16, :])

    total, value = exchange(SA, RA, pi, prim, 0, D)
    extra = split(value)
    for m in range(4):
        SB[m, 0:192, :] = total[m * 192:(m + 1) * 192, :].astype(BF)
        SB[m, 192:208, :] = extra
    total, value = exchange(SB, RB, si, sec, 3, 192)
    extra = split(value)
    for m in range(4):
        SC[m, 0:48, :] = total[m * 48:(m + 1) * 48, :]
        SC[m, 48:64, :] = extra.astype(F32)
    total, value = exchange(SC, RC, g, zed, 6, 48)

    EX[c] = split(value)
    send(EX.at[c], EX.at[c], ms.at[2], mr.at[2], sib)

    def spread(ring, base, row_of, rows):
        ref = grads.at[c, pl.ds(row_of(0), rows)]
        for k in (1, 2, 3):
            send(ref, ref, gs.at[base + k], gr.at[base + k], ring(k))
        for k in (1, 2, 3):
            landed(grads.at[c, pl.ds(row_of(-k), rows)], gs.at[base + k], gr.at[base + k])

    def at(p, s, z):
        return ((pi + p + 4) % 4) * 768 + ((si + s + 4) % 4) * 192 + ((g + z + 4) % 4) * 48

    grads[c, pl.ds(at(0, 0, 0), 48), :] = total.astype(BF)
    spread(zed, 9, lambda k: at(0, 0, k), 48)
    spread(sec, 12, lambda k: pi * 768 + ((si + k + 4) % 4) * 192, 192)

    def block(k, cc=None):
        which = c if cc is None else cc
        index = x * (1 - which) + y * which
        return grads.at[which, pl.ds(((index + k + 4) % 4) * 768, 768)]

    for k in (1, 2, 3):
        send(block(0), block(0), gs.at[15 + k], gr.at[15 + k], prim(k))
    send(block(0), block(0), ms.at[3], mr.at[3], sib)
    for k in (1, 2, 3):
        landed(block(-k), gs.at[15 + k], gr.at[15 + k])
        send(block(-k), block(-k), ms.at[3 + k], mr.at[3 + k], sib)
    landed(EX.at[1 - c], ms.at[2], mr.at[2])
    extra_out[...] = join(EX[0].astype(F32)) + join(EX[1].astype(F32))
    for k in range(4):
        landed(block(-k, 1 - c), ms.at[3 + k], mr.at[3 + k])
    for cp in pending:
        cp.wait_send()


def finish(emb_in, grads, extra, emb, loss, grad_self, grad_nbr, grad_bias):
    emb[...] = emb_in[...]
    loss[...] = extra[4:5, 0:1] * (1.0 / NODES)
    for m in range(4):
        at = slice(m * 128, (m + 1) * 128)
        grad_self[:, at] = grads[0, m * D:(m + 1) * D, :].astype(F32)
        grad_nbr[:, at] = grads[1, m * D:(m + 1) * D, :].astype(F32)
        grad_bias[:, at] = extra[m:m + 1, :]


def shards(features, text_embed, adjacency, block_cols, positive, self_weight, nbr_weight, hidden_bias):
    vmem = pl.BlockSpec(memory_space=pltpu.VMEM)
    smem = pl.BlockSpec(memory_space=pltpu.SMEM)
    hbm = pl.BlockSpec(memory_space=pl.ANY)
    dma = pltpu.SemaphoreType.DMA
    emb, grads, extra = pl.pallas_call(
        kernel,
        name="step",
        out_shape=(
            jax.ShapeDtypeStruct((ROWS, H), BF),
            jax.ShapeDtypeStruct((2, 4 * D, 128), BF),
            jax.ShapeDtypeStruct((8, 128), F32),
        ),
        in_specs=[vmem, vmem, hbm, smem, vmem, hbm, hbm, vmem],
        out_specs=(vmem, vmem, vmem),
        scratch_shapes=[
            pltpu.VMEM((SLAB + N_GRP * ROWS, D), BF),
            pltpu.VMEM((SLAB, H), BF),
            pltpu.VMEM((N_GRP, ROWS, H), BF),
            pltpu.VMEM((N_GRP, 8, ROWS), F32),
            pltpu.VMEM((N_GRP * ROWS, 128), F32),
            pltpu.VMEM((2 * ROWS, D), BF),
            pltpu.VMEM((ROWS, H), F32),
            pltpu.VMEM((2 * ROWS, H), BF),
            pltpu.VMEM((D, 2 * ROWS), BF),
            pltpu.VMEM((ROWS, H), F32),
            pltpu.VMEM((ROWS, 128), F32),
            pltpu.VMEM((ROWS, H), F32),
            pltpu.VMEM((ROWS, 128), F32),
            pltpu.VMEM((N_GRP * ROWS, H), BF),
            pltpu.VMEM((3, ROWS, H), BF),
            pltpu.VMEM((3, ROWS, H), BF),
            pltpu.VMEM((3, ROWS, H), BF),
            pltpu.VMEM((3, 8, ROWS), F32),
            pltpu.VMEM((3, 8, ROWS), F32),
            pltpu.VMEM((4, D + 16, 128), BF),
            pltpu.VMEM((3, D + 16, 128), BF),
            pltpu.VMEM((4, 208, 128), BF),
            pltpu.VMEM((3, 208, 128), BF),
            pltpu.VMEM((4, 64, 128), F32),
            pltpu.VMEM((3, 64, 128), F32),
            pltpu.VMEM((2, 16, 128), BF),
            pltpu.VMEM((ROWS, K * BLOCK), BF),
            pltpu.VMEM((D, H), BF),
            pltpu.VMEM((D, H), BF),
            dma((GATHER_SEMS,)), dma((GATHER_SEMS,)),
            dma((GATHER_SEMS,)), dma((GATHER_SEMS,)),
            dma((18,)), dma((18,)),
            dma((7,)), dma((7,)),
            dma((19,)), dma((19,)),
            dma((3,)),
        ],
        compiler_params=pltpu.CompilerParams(
            collective_id=0, has_side_effects=True, vmem_limit_bytes=56 * 2**20
        ),
        cost_estimate=pl.CostEstimate(
            flops=30 * 10**9, bytes_accessed=8 * 2**20, transcendentals=8 * 2**20
        ),
    )(
        features, text_embed, adjacency, block_cols, positive.reshape(1, ROWS), self_weight, nbr_weight,
        hidden_bias.reshape(1, H),
    )
    emb, loss, grad_self, grad_nbr, grad_bias = pl.pallas_call(
        finish,
        name="finish",
        out_shape=(
            jax.ShapeDtypeStruct((ROWS, H), BF),
            jax.ShapeDtypeStruct((1, 1), F32),
            jax.ShapeDtypeStruct((D, H), F32),
            jax.ShapeDtypeStruct((D, H), F32),
            jax.ShapeDtypeStruct((1, H), F32),
        ),
        in_specs=[vmem] * 3,
        out_specs=(vmem,) * 5,
    )(emb, grads, extra)
    return emb, loss.reshape(()), grad_self, grad_nbr, grad_bias.reshape(H)


def solution(mesh):
    rows = P(("grp", "dom"), None)
    return jax.shard_map(
        shards,
        mesh=mesh,
        in_specs=(rows, rows, rows, rows, P(("grp", "dom")), P(), P(), P()),
        out_specs=(rows, P(), P(), P(), P()),
        check_vma=False,
    )
```

```python
import jax
import jax.numpy as jnp
from jax import lax
from jax.experimental import pallas as pl
from jax.experimental.pallas import tpu as pltpu
from jax.sharding import PartitionSpec as P

MESH = pl.DeviceIdType.MESH
D = 768
H = 512
BLOCK = 128
K = 8
ROWS = 256
HALF = 128
N_GRP = 4
N_DOM = 32
NODES = 32768
SLAB = N_DOM * ROWS
WIDE = 1024
STRIP = 64

EPS = 1e-05
SCALE = 10.0 / H
LOG2E = 1.4426950408889634

BF = jnp.bfloat16
F32 = jnp.float32

ORDER = (
    (-1, 0, 0), (1, 0, 1), (-1, 0, 1), (1, 0, 0), (0, -1, 0), (0, 1, 0), (0, -1, 1), (0, 1, 1),
    (2, 0, 0), (-1, 1, 0), (-1, -1, 0), (2, 0, 1), (1, -1, 1), (1, 1, 1), (-1, -1, 1), (-1, 1, 1),
    (1, -1, 0), (1, 1, 0), (0, 2, 0), (0, 2, 1), (2, -1, 0), (2, 1, 0), (-1, 2, 0), (2, 1, 1),
    (2, -1, 1), (1, 2, 1), (-1, 2, 1), (1, 2, 0), (2, 2, 0), (2, 2, 1),
)
SHARDS = (
    (0, 0), (-1, 0), (1, 0), (0, -1), (0, 1), (2, 0), (-1, -1), (-1, 1),
    (1, -1), (1, 1), (0, 2), (2, -1), (2, 1), (-1, 2), (1, 2), (2, 2),
)
UNITS = (7, 15, 24, 29)
GATHER_SEMS = len(ORDER) + len(SHARDS)


def rms_scale(values):
    return lax.rsqrt(jnp.mean(values * values, axis=1, keepdims=True) + EPS)


def dot(a, b):
    return jnp.dot(a, b, preferred_element_type=F32)


def dot_nt(a, b):
    return lax.dot_general(a, b, (((1,), (1,)), ((), ())), preferred_element_type=F32)


def column(row):
    return jnp.transpose(jnp.broadcast_to(row, (128, ROWS)))


def lane_sums(a):
    return lax.dot_general(
        jnp.ones((8, 128), F32), a, (((1,), (1,)), ((), ())),
        precision=lax.Precision.HIGHEST, preferred_element_type=F32,
    )


def split(v):
    high = v.astype(BF).astype(F32)
    return jnp.concatenate([high, v - high], axis=0).astype(BF)


def join(pair):
    return pair[0:8, :] + pair[8:16, :]


def kernel(
    feat_h, text_h, adj_h, cols_h, pos_h, self_h, nbr_h, bias_h,
    emb_h, grads_h, extra_h,
    FE, T, Q, POS, PCOL, AGG, HID, G, LT, TACC, PACC, RT, W_S, W_R, W_O, TP_S, TP_R,
    SA, RA, SB, RB, EX, GR, XO,
    text, adj, cols, pos, self_w, nbr_w, bias, emb,
    fs, fr, ts, tr, zs, zr, ms, mr, gs, gr, ls,
):
    g = lax.axis_index("grp")
    d = lax.axis_index("dom")
    c = d % 2
    x = (d // 2) % 4
    y = d // 8

    def dom_at(i, j, cc):
        ux, uy = 1 - cc, cc
        ax = (x + i * ux + j * uy + 4) % 4
        ay = (y + i * uy + j * ux + 4) % 4
        return (ay * 4 + ax) * 2 + cc

    def prim(k):
        return (g, dom_at(k, 0, c))

    def sec(k):
        return (g, dom_at(0, k, c))

    def zed(k):
        return ((g + k) % 4, d)

    def wall(j, k):
        return ((g + k) % 4, dom_at(0, j, c))

    sib = (g, d + 1 - 2 * c)
    pi = x * (1 - c) + y * c
    si = x * c + y * (1 - c)
    F = FE.at[:, pl.ds(0, D)]

    barrier = pltpu.get_barrier_semaphore()
    across = [(j, k) for j in range(4) for k in range(4) if j or k]
    partners = [sib] + [prim(k) for k in (1, 2, 3)] + [wall(j, k) for j, k in across]
    for dev in partners:
        pl.semaphore_signal(barrier, inc=1, device_id=dev, device_id_type=MESH)

    own = pl.ds(d * ROWS, ROWS)
    loads = [
        pltpu.make_async_copy(src, dst, ls.at[n])
        for n, (src, dst) in enumerate((
            (text_h, text), (pos_h, pos), (feat_h, F.at[own]), (cols_h, cols), (bias_h, bias),
            (adj_h, adj), (self_h, self_w), (nbr_h, nbr_w),
        ))
    ]
    for load in loads:
        load.start()

    pending = []
    feature_sends = []

    def rcopy(src, dst, ssem, rsem, dev):
        return pltpu.make_async_remote_copy(
            src_ref=src, dst_ref=dst, send_sem=ssem, recv_sem=rsem,
            device_id=dev, device_id_type=MESH,
        )

    def send(src, dst, ssem, rsem, dev, kept=pending):
        cp = rcopy(src, dst, ssem, rsem, dev)
        cp.start()
        kept.append(cp)

    def landed(region, ssem, rsem):
        rcopy(region, region, ssem, rsem, sib).wait_recv()

    def drain(kept):
        for cp in kept:
            cp.wait_send()

    class Gather:
        def __init__(self, tab, ssem, rsem, kept):
            self.tab, self.ss, self.rs, self.kept = tab, ssem, rsem, kept
            self.here = set()
            self.done = 0

        def shard(self, i, j, cc, half=None):
            base = dom_at(i, j, cc) * ROWS
            if half is None:
                return self.tab.at[pl.ds(base, ROWS)]
            return self.tab.at[pl.ds(base + half * HALF, HALF)]

        def send(self, key, to, dev):
            ref = self.shard(key[0], key[1], c, key[2])
            k = ORDER.index(to + (key[2],))
            send(ref, ref, self.ss.at[k], self.rs.at[k], dev, self.kept)

        def across(self, i, j):
            ref = self.shard(i, j, c)
            k = len(ORDER) + SHARDS.index((i, j))
            send(ref, ref, self.ss.at[k], self.rs.at[k], sib, self.kept)

        def along(self, i, h):
            self.send((i, 0, h), (i, -1), sec(1))
            self.send((i, 0, h), (i, 1), sec(-1))

        def start(self):
            self.send((0, 0, 0), (-1, 0), prim(1))
            self.send((0, 0, 1), (1, 0), prim(-1))
            self.send((0, 0, 1), (-1, 0), prim(1))
            self.send((0, 0, 0), (1, 0), prim(-1))
            self.along(0, 0)
            self.along(0, 1)
            self.across(0, 0)

        def to(self, last):
            while self.done <= last:
                self.step(self.done)
                self.done += 1

        def step(self, n):
            i, j, h = key = ORDER[n]
            landed(self.shard(i, j, c, h), self.ss.at[n], self.rs.at[n])
            if key == (-1, 0, 0):
                self.send(key, (2, 0), prim(1))
            if key == (1, 0, 1):
                self.send(key, (2, 0), prim(-1))
            if j == 0:
                self.along(i, h)
            if j == -1 and h == 0:
                self.send(key, (i, 2), sec(1))
            if j == 1 and h == 1:
                self.send(key, (i, 2), sec(-1))
            if (i, j) in self.here:
                self.across(i, j)
            self.here.add((i, j))

        def sibling(self, i, j):
            k = len(ORDER) + SHARDS.index((i, j))
            landed(self.shard(i, j, 1 - c), self.ss.at[k], self.rs.at[k])

    gf = Gather(F, fs, fr, feature_sends)
    gt = Gather(T, ts, tr, pending)

    loads[0].wait()
    tw = text[...].astype(F32)
    T[own, :] = (tw * rms_scale(tw)).astype(BF)
    loads[1].wait()
    POS[g] = jnp.broadcast_to(pos[...].astype(F32), (8, ROWS))
    loads[2].wait()
    pl.semaphore_wait(barrier, len(partners))

    gf.start()
    mine = F.at[pl.ds(SLAB + g * ROWS, ROWS)]
    for k in (1, 3, 2):
        send(F.at[own], mine, zs.at[k - 1], zr.at[k - 1], zed(k), feature_sends)
        send(POS.at[g], POS.at[g], zs.at[k + 2], zr.at[k + 2], zed(k))
    gf.to(24)
    gt.start()
    gf.to(29)
    gt.to(3)
    for i, j in SHARDS:
        gf.sibling(i, j)

    def from_zed(k):
        return (g - k + 4) % 4

    for k in (1, 2, 3):
        o = from_zed(k)
        landed(F.at[pl.ds(SLAB + o * ROWS, ROWS)], zs.at[k - 1], zr.at[k - 1])

    for load in loads[3:]:
        load.wait()
    for r in range(2):
        rows = pl.ds(r * BLOCK, BLOCK)
        agg = jnp.zeros((BLOCK, D), F32)
        for k in range(K):
            b = cols[r, k]
            device = b // 2
            group, domain = device // N_DOM, device % N_DOM
            at = jnp.where(group == g, domain * 2 + b % 2, SLAB // BLOCK + group * 2 + b % 2)
            agg = agg + dot(adj[rows, k * BLOCK:(k + 1) * BLOCK], F[pl.ds(at * BLOCK, BLOCK), :])
        high = agg.astype(BF)
        rest = agg - high.astype(F32)
        low = rest.astype(BF)
        lowest = (rest - low.astype(F32)).astype(BF)
        AGG[pl.ds(c * ROWS + r * BLOCK, BLOCK), :] = high
        pre = (
            dot(F[pl.ds(d * ROWS + r * BLOCK, BLOCK), :], self_w[...])
            + (dot(high, nbr_w[...]) + (dot(low, nbr_w[...]) + dot(lowest, nbr_w[...])))
            + bias[...]
        )
        hidden = jnp.maximum(pre, 0.0)
        HID[rows, :] = hidden
        emb[rows, :] = hidden.astype(BF)
        Q[g, rows, :] = (hidden * rms_scale(hidden)).astype(BF)
        gt.to(5 + 2 * r)

    for k in (1, 3):
        send(Q.at[g], Q.at[g], zs.at[k + 5], zr.at[k + 5], zed(k))
    agg_own = AGG.at[pl.ds(c * ROWS, ROWS)]
    send(agg_own, agg_own, ms.at[0], mr.at[0], sib)
    emb_out = pltpu.make_async_copy(emb, emb_h, ls.at[8])
    emb_out.start()

    for k in (1, 2, 3):
        o = from_zed(k)
        landed(POS.at[o], zs.at[k + 2], zr.at[k + 2])
    lanes = lax.broadcasted_iota(jnp.int32, (ROWS, 128), 1).astype(F32)
    for o in range(N_GRP):
        PCOL[o] = column(POS[o, 0:1, :]) - lanes
    TACC[...] = jnp.zeros_like(TACC)
    PACC[...] = jnp.zeros_like(PACC)
    sib_rows = pl.ds((1 - c) * ROWS, ROWS)
    landed(AGG.at[sib_rows], ms.at[0], mr.at[0])
    pair = F[pl.ds((d // 2) * 2 * ROWS, 2 * ROWS), :]
    LT[...] = jnp.transpose(jnp.where(c == 0, pair, AGG[...]))
    drain(feature_sends)

    def doms_of(u, v):
        return [dom_at(i, j, c if v == 0 else 1 - c) for i, j in SHARDS[4 * u:4 * u + 4]]

    def offsets(dom):
        return [(g * SLAB + dom * ROWS + m * 128).astype(F32) for m in range(ROWS // 128)]

    def texts(u):
        doms = doms_of(u, 0) + doms_of(u, 1)
        ats = [at for dom in doms for at in offsets(dom)]
        return jnp.concatenate([T[pl.ds(dom * ROWS, ROWS), :] for dom in doms], axis=0), ats

    def exponentials(o, u):
        part, ats = texts(u)
        logits = dot_nt(Q[o], part)
        for r in range(0, ROWS, STRIP):
            rows = slice(r, r + STRIP)
            tot, picked, where = TACC[o, rows, :], PACC[o, rows, :], PCOL[o, rows, :]
            for m, at in enumerate(ats):
                tile = logits[rows, m * 128:(m + 1) * 128]
                e = jnp.exp2(tile * (SCALE * LOG2E))
                tot = tot + e
                picked = picked + jnp.where(where == at, tile, 0.0)
                lane = (m % 8) * 128
                base = (u * 2 + m // 8) * WIDE + o * ROWS + r
                FE[pl.ds(base, STRIP), lane:lane + 128] = e.astype(BF)
            TACC[o, rows, :] = tot
            PACC[o, rows, :] = picked

    def arrive(u):
        gt.to(UNITS[u])
        for i, j in SHARDS[4 * u:4 * u + 4]:
            gt.sibling(i, j)

    def queries(k):
        o = (g + k) % 4
        landed(Q.at[o], zs.at[9 - k], zr.at[9 - k])

    arrive(0)
    exponentials(g, 0)
    gt.to(11)
    arrive(1)
    send(Q.at[g], Q.at[g], zs.at[7], zr.at[7], zed(2))
    exponentials(g, 1)
    gt.to(17)
    for k, last in ((1, 19), (3, 23)):
        queries(k)
        for u in (0, 1):
            exponentials((g + k) % 4, u)
            gt.to(last + 2 * u if k == 1 else min(24, last + u))
    gt.to(24)
    arrive(2)
    for k in (0, 1, 3):
        exponentials((g + k) % 4, 2)
    queries(2)
    for u in range(3):
        exponentials((g + 2) % 4, u)
        gt.to((27, 29, 29)[u])
    arrive(3)
    for o in range(N_GRP):
        exponentials(o, 3)
        TP_S[o, 0:8, :] = lane_sums(TACC[o])
        TP_S[o, 8:16, :] = lane_sums(PACC[o])
        for k in (1, 2, 3):
            n = 8 + 4 * k + o - 3
            send(TP_S.at[o], TP_R.at[k - 1, o], zs.at[n], zr.at[n], zed(k))

    def totals(o):
        rows = TP_S[o]
        for k in (1, 2, 3):
            n = 8 + 4 * k + o - 3
            landed(TP_R.at[k - 1, o], zs.at[n], zr.at[n])
            rows = rows + TP_R[k - 1, o]
        return rows

    index = lax.broadcasted_iota(jnp.int32, (ROWS, 128), 0) % 64
    factor = 1.0 + (2 * index + 1).astype(F32) * (1.0 / 128)

    for o in range(N_GRP):
        rows = totals(o)
        RT[o] = factor / column(rows[0:1, :])
        TACC[o, 0:16, :] = rows[:, 0:128]
        TACC[o, 16:32, :] = rows[:, 128:256]

    def weigh(o, half):
        acc = jnp.zeros((HALF, H), F32)
        for u in range(4):
            part, ats = texts(u)
            strips = []
            for r in range(half * HALF, (half + 1) * HALF, STRIP):
                rows = slice(r, r + STRIP)
                inverse, where, unit = RT[o, rows, :], PCOL[o, rows, :], factor[rows, :]
                tiles = []
                for m, at in enumerate(ats):
                    lane = (m % 8) * 128
                    base = (u * 2 + m // 8) * WIDE + o * ROWS + r
                    e = FE[pl.ds(base, STRIP), lane:lane + 128]
                    w = e.astype(F32) * inverse
                    tiles.append((w - jnp.where(where == at, unit, 0.0)).astype(BF))
                strips.append(jnp.concatenate(tiles, axis=1))
            acc = acc + dot(jnp.concatenate(strips, axis=0), part)
        return acc

    for j in range(3):
        o = j + jnp.where(j < g, 0, 1)
        k = (o - g + 4) % 4
        for half in range(2):
            at = pl.ds(half * HALF, HALF)
            W_S[j, at, :] = weigh(o, half).astype(BF)
            send(
                W_S.at[j, at], W_R.at[k - 1, at],
                zs.at[21 + 2 * j + half], zr.at[19 + 2 * k + half], (o, d),
            )
    for half in range(2):
        W_O[pl.ds(half * HALF, HALF), :] = weigh(g, half)

    for k in (1, 2, 3):
        for half in range(2):
            n = 19 + 2 * k + half
            landed(W_R.at[k - 1, pl.ds(half * HALF, HALF)], zs.at[n], zr.at[n])

    unit = W_O[...]
    for k in range(3):
        unit = unit + W_R[k].astype(F32)
    unit = unit * (SCALE / factor[:, 0:1])
    lane_parts = jnp.concatenate([TACC[g, 0:16, :], TACC[g, 16:32, :]], axis=1)
    loss = jnp.sum(
        jnp.log(lane_parts[0:1, :]) - SCALE * lane_parts[8:9, :], axis=1, keepdims=True
    )
    hidden = HID[...]
    scale_rows = rms_scale(hidden)
    normed = hidden * scale_rows
    back = scale_rows * (unit - normed * jnp.mean(unit * normed, axis=1, keepdims=True))
    grad_pre = jnp.where(hidden > 0, back, 0.0)
    G[pl.ds(c * ROWS, ROWS), :] = grad_pre.astype(BF)
    g_own = G.at[pl.ds(c * ROWS, ROWS)]
    send(g_own, g_own, ms.at[1], mr.at[1], sib)

    bias_sum = jnp.sum(grad_pre, axis=0, keepdims=True)
    parts = [bias_sum[:, m * 128:(m + 1) * 128] for m in range(4)]
    parts.append(jnp.broadcast_to(loss, (1, 128)))
    parts.append(jnp.zeros((3, 128), F32))
    extra = split(jnp.concatenate(parts, axis=0))

    landed(G.at[sib_rows], ms.at[1], mr.at[1])

    for k in (1, 3, 2, 0):
        m = (pi + k) % 4
        columns = pl.ds(pl.multiple_of(m * 128, 128), 128)
        SA[m, 0:D, :] = dot(LT[...], G[:, columns]).astype(BF)
        SA[m, D:D + 16, :] = extra
        if k:
            send(SA.at[m], RA.at[k - 1], gs.at[k - 1], gr.at[k - 1], prim(k))
    total = SA[pi].astype(F32)
    for k in (1, 3, 2):
        landed(RA.at[k - 1], gs.at[k - 1], gr.at[k - 1])
        total = total + RA[k - 1].astype(F32)
    extra = split(join(total[D:D + 16, :]))

    for m in range(16):
        SB[m, 0:48, :] = total[m * 48:(m + 1) * 48, :].astype(BF)
        SB[m, 48:64, :] = extra
    me = si * 4 + g
    for n, (j, k) in enumerate(across):
        m = ((si + j) % 4) * 4 + (g + k) % 4
        send(SB.at[m], RB.at[n], gs.at[3 + n], gr.at[3 + n], wall(j, k))
    total = SB[me].astype(F32)
    for n in range(15):
        landed(RB.at[n], gs.at[3 + n], gr.at[3 + n])
        total = total + RB[n].astype(F32)

    EX[c] = split(join(total[48:64, :]))
    send(EX.at[c], EX.at[c], ms.at[2], mr.at[2], sib)

    def piece(j, k):
        return GR.at[c, pl.ds(pi * 768 + ((si + j + 4) % 4) * 192 + ((g + k + 4) % 4) * 48, 48)]

    GR[c, pl.ds(pi * 768 + si * 192 + g * 48, 48), :] = total[0:48, :].astype(BF)
    for n, (j, k) in enumerate(across):
        send(piece(0, 0), piece(0, 0), gs.at[18 + n], gr.at[18 + n], wall(j, k))
    for n, (j, k) in enumerate(across):
        landed(piece(-j, -k), gs.at[18 + n], gr.at[18 + n])

    def block(k, cc):
        index = x * (1 - cc) + y * cc
        return ((index + k + 4) % 4) * 768

    def both(k, cc):
        return GR.at[cc, pl.ds(block(k, cc), 768)]

    outs = []

    def write(k, cc):
        at = pl.ds(block(k, cc), 768)
        cp = pltpu.make_async_copy(GR.at[cc, at], grads_h.at[cc, at], ls.at[9 + len(outs)])
        cp.start()
        outs.append(cp)

    for k in (1, 3, 2):
        send(both(0, c), both(0, c), gs.at[32 + k], gr.at[32 + k], prim(k))
    send(both(0, c), both(0, c), ms.at[3], mr.at[3], sib)
    write(0, c)
    landed(EX.at[1 - c], ms.at[2], mr.at[2])
    XO[...] = join(EX[0].astype(F32)) + join(EX[1].astype(F32))
    extra_out = pltpu.make_async_copy(XO, extra_h, ls.at[17])
    extra_out.start()
    for k in (1, 3, 2):
        landed(both(-k, c), gs.at[32 + k], gr.at[32 + k])
        send(both(-k, c), both(-k, c), ms.at[3 + k], mr.at[3 + k], sib)
        write(-k, c)
    for k in (0, 1, 3, 2):
        landed(both(-k, 1 - c), ms.at[3 + k], mr.at[3 + k])
        write(-k, 1 - c)
    for cp in outs:
        cp.wait()
    emb_out.wait()
    extra_out.wait()
    drain(pending)


def finish(emb_in, grads, extra, emb, loss, grad_self, grad_nbr, grad_bias):
    emb[...] = emb_in[...]
    loss[...] = extra[4:5, 0:1] * (1.0 / NODES)
    for m in range(4):
        at = slice(m * 128, (m + 1) * 128)
        grad_self[:, at] = grads[0, m * D:(m + 1) * D, :].astype(F32)
        grad_nbr[:, at] = grads[1, m * D:(m + 1) * D, :].astype(F32)
        grad_bias[:, at] = extra[m:m + 1, :]


def shards(features, text_embed, adjacency, block_cols, positive, self_weight, nbr_weight, hidden_bias):
    vmem = pl.BlockSpec(memory_space=pltpu.VMEM)
    hbm = pl.BlockSpec(memory_space=pl.ANY)
    dma = pltpu.SemaphoreType.DMA
    emb, grads, extra = pl.pallas_call(
        kernel,
        name="step",
        out_shape=(
            jax.ShapeDtypeStruct((ROWS, H), BF),
            jax.ShapeDtypeStruct((2, 4 * D, 128), BF),
            jax.ShapeDtypeStruct((8, 128), F32),
        ),
        in_specs=[hbm] * 8,
        out_specs=(hbm,) * 3,
        scratch_shapes=[
            pltpu.VMEM((SLAB + N_GRP * ROWS, WIDE), BF),
            pltpu.VMEM((SLAB, H), BF),
            pltpu.VMEM((N_GRP, ROWS, H), BF),
            pltpu.VMEM((N_GRP, 8, ROWS), F32),
            pltpu.VMEM((N_GRP, ROWS, 128), F32),
            pltpu.VMEM((2 * ROWS, D), BF),
            pltpu.VMEM((ROWS, H), F32),
            pltpu.VMEM((2 * ROWS, H), BF),
            pltpu.VMEM((D, 2 * ROWS), BF),
            pltpu.VMEM((N_GRP, ROWS, 128), F32),
            pltpu.VMEM((N_GRP, ROWS, 128), F32),
            pltpu.VMEM((N_GRP, ROWS, 128), F32),
            pltpu.VMEM((3, ROWS, H), BF),
            pltpu.VMEM((3, ROWS, H), BF),
            pltpu.VMEM((ROWS, H), F32),
            pltpu.VMEM((N_GRP, 16, ROWS), F32),
            pltpu.VMEM((3, N_GRP, 16, ROWS), F32),
            pltpu.VMEM((4, D + 16, 128), BF),
            pltpu.VMEM((3, D + 16, 128), BF),
            pltpu.VMEM((16, 64, 128), BF),
            pltpu.VMEM((15, 64, 128), BF),
            pltpu.VMEM((2, 16, 128), BF),
            pltpu.VMEM((2, 4 * D, 128), BF),
            pltpu.VMEM((8, 128), F32),
            pltpu.VMEM((ROWS, H), BF),
            pltpu.VMEM((ROWS, K * BLOCK), BF),
            pltpu.SMEM((2, K), jnp.int32),
            pltpu.VMEM((1, ROWS), jnp.int32),
            pltpu.VMEM((D, H), BF),
            pltpu.VMEM((D, H), BF),
            pltpu.VMEM((1, H), F32),
            pltpu.VMEM((ROWS, H), BF),
            dma((GATHER_SEMS,)), dma((GATHER_SEMS,)),
            dma((GATHER_SEMS,)), dma((GATHER_SEMS,)),
            dma((30,)), dma((30,)),
            dma((7,)), dma((7,)),
            dma((36,)), dma((36,)),
            dma((18,)),
        ],
        compiler_params=pltpu.CompilerParams(
            collective_id=0, has_side_effects=True, vmem_limit_bytes=56 * 2**20
        ),
        cost_estimate=pl.CostEstimate(
            flops=20 * 10**9, bytes_accessed=8 * 2**20, transcendentals=8 * 2**20
        ),
    )(
        features, text_embed, adjacency, block_cols, positive.reshape(1, ROWS), self_weight,
        nbr_weight, hidden_bias.reshape(1, H),
    )
    emb, loss, grad_self, grad_nbr, grad_bias = pl.pallas_call(
        finish,
        name="finish",
        out_shape=(
            jax.ShapeDtypeStruct((ROWS, H), BF),
            jax.ShapeDtypeStruct((1, 1), F32),
            jax.ShapeDtypeStruct((D, H), F32),
            jax.ShapeDtypeStruct((D, H), F32),
            jax.ShapeDtypeStruct((1, H), F32),
        ),
        in_specs=[vmem] * 3,
        out_specs=(vmem,) * 5,
    )(emb, grads, extra)
    return emb, loss.reshape(()), grad_self, grad_nbr, grad_bias.reshape(H)


def solution(mesh):
    rows = P(("grp", "dom"), None)
    return jax.shard_map(
        shards,
        mesh=mesh,
        in_specs=(rows, rows, rows, rows, P(("grp", "dom")), P(), P(), P()),
        out_specs=(rows, P(), P(), P(), P()),
        check_vma=False,
    )
```

```python
import jax
import jax.numpy as jnp
from jax import lax
from jax.experimental import pallas as pl
from jax.experimental.pallas import tpu as pltpu
from jax.sharding import PartitionSpec as P

MESH = pl.DeviceIdType.MESH
D = 768
H = 512
BLOCK = 128
K = 8
ROWS = 256
HALF = 128
N_GRP = 4
N_DOM = 32
NODES = 32768
SLAB = N_DOM * ROWS
WIDE = 1024
STRIP = 64

EPS = 1e-05
SCALE = 10.0 / H
LOG2E = 1.4426950408889634

BF = jnp.bfloat16
F32 = jnp.float32

ORDER = (
    (-1, 0, 0), (1, 0, 1), (-1, 0, 1), (1, 0, 0), (0, -1, 0), (0, 1, 0), (0, -1, 1), (0, 1, 1),
    (2, 0, 0), (-1, 1, 0), (-1, -1, 0), (2, 0, 1), (1, -1, 1), (1, 1, 1), (-1, -1, 1), (-1, 1, 1),
    (1, -1, 0), (1, 1, 0), (0, 2, 0), (0, 2, 1), (2, -1, 0), (2, 1, 0), (-1, 2, 0), (2, 1, 1),
    (2, -1, 1), (1, 2, 1), (-1, 2, 1), (1, 2, 0), (2, 2, 0), (2, 2, 1),
)
SHARDS = (
    (0, 0), (-1, 0), (1, 0), (0, -1), (0, 1), (2, 0), (-1, -1), (-1, 1),
    (1, -1), (1, 1), (0, 2), (2, -1), (2, 1), (-1, 2), (1, 2), (2, 2),
)
UNITS = (7, 15, 24, 29)
GATHER_SEMS = len(ORDER) + len(SHARDS)


def rms_scale(values):
    return lax.rsqrt(jnp.mean(values * values, axis=1, keepdims=True) + EPS)


def dot(a, b):
    return jnp.dot(a, b, preferred_element_type=F32)


def dot_nt(a, b):
    return lax.dot_general(a, b, (((1,), (1,)), ((), ())), preferred_element_type=F32)


def column(row):
    return jnp.transpose(jnp.broadcast_to(row, (128, ROWS)))


def lane_sums(a):
    return jnp.sum(jnp.transpose(a), axis=0, keepdims=True)


def split(v):
    high = v.astype(BF).astype(F32)
    return jnp.concatenate([high, v - high], axis=0).astype(BF)


def join(pair):
    return pair[0:8, :] + pair[8:16, :]


def kernel(
    feat_h, text_h, adj_h, cols_h, pos_h, self_h, nbr_h, bias_h,
    emb_h, grads_h, extra_h,
    FE, T, Q, POS, PCOL, AGG, HID, G, LT, TACC, PACC, RT, W_S, W_R, W_O, TP_S, TP_R,
    SA, RA, SB, RB, EX, GR, XO,
    text, adj, cols, pos, self_w, nbr_w, bias, emb,
    fs, fr, ts, tr, zs, zr, ms, mr, gs, gr, ls,
):
    g = lax.axis_index("grp")
    d = lax.axis_index("dom")
    c = d % 2
    x = (d // 2) % 4
    y = d // 8

    def dom_at(i, j, cc):
        ux, uy = 1 - cc, cc
        ax = (x + i * ux + j * uy + 4) % 4
        ay = (y + i * uy + j * ux + 4) % 4
        return (ay * 4 + ax) * 2 + cc

    def prim(k):
        return (g, dom_at(k, 0, c))

    def sec(k):
        return (g, dom_at(0, k, c))

    def zed(k):
        return ((g + k) % 4, d)

    def wall(j, k):
        return ((g + k) % 4, dom_at(0, j, c))

    sib = (g, d + 1 - 2 * c)
    pi = x * (1 - c) + y * c
    si = x * c + y * (1 - c)
    F = FE.at[:, pl.ds(0, D)]

    barrier = pltpu.get_barrier_semaphore()
    across = [(j, k) for j in range(4) for k in range(4) if j or k]
    partners = [sib] + [prim(k) for k in (1, 2, 3)] + [wall(j, k) for j, k in across]
    for dev in partners:
        pl.semaphore_signal(barrier, inc=1, device_id=dev, device_id_type=MESH)

    own = pl.ds(d * ROWS, ROWS)
    loads = [
        pltpu.make_async_copy(src, dst, ls.at[n])
        for n, (src, dst) in enumerate((
            (text_h, text), (pos_h, pos), (feat_h, F.at[own]), (cols_h, cols), (bias_h, bias),
            (adj_h, adj), (self_h, self_w), (nbr_h, nbr_w),
        ))
    ]
    for load in loads:
        load.start()

    pending = []
    feature_sends = []

    def rcopy(src, dst, ssem, rsem, dev):
        return pltpu.make_async_remote_copy(
            src_ref=src, dst_ref=dst, send_sem=ssem, recv_sem=rsem,
            device_id=dev, device_id_type=MESH,
        )

    def send(src, dst, ssem, rsem, dev, kept=pending):
        cp = rcopy(src, dst, ssem, rsem, dev)
        cp.start()
        kept.append(cp)

    def landed(region, ssem, rsem):
        rcopy(region, region, ssem, rsem, sib).wait_recv()

    def drain(kept):
        for cp in kept:
            cp.wait_send()

    class Gather:
        def __init__(self, tab, ssem, rsem, kept):
            self.tab, self.ss, self.rs, self.kept = tab, ssem, rsem, kept
            self.here = set()
            self.done = 0

        def shard(self, i, j, cc, half=None):
            base = dom_at(i, j, cc) * ROWS
            if half is None:
                return self.tab.at[pl.ds(base, ROWS)]
            return self.tab.at[pl.ds(base + half * HALF, HALF)]

        def send(self, key, to, dev):
            ref = self.shard(key[0], key[1], c, key[2])
            k = ORDER.index(to + (key[2],))
            send(ref, ref, self.ss.at[k], self.rs.at[k], dev, self.kept)

        def across(self, i, j):
            ref = self.shard(i, j, c)
            k = len(ORDER) + SHARDS.index((i, j))
            send(ref, ref, self.ss.at[k], self.rs.at[k], sib, self.kept)

        def along(self, i, h):
            self.send((i, 0, h), (i, -1), sec(1))
            self.send((i, 0, h), (i, 1), sec(-1))

        def start(self):
            self.send((0, 0, 0), (-1, 0), prim(1))
            self.send((0, 0, 1), (1, 0), prim(-1))
            self.send((0, 0, 1), (-1, 0), prim(1))
            self.send((0, 0, 0), (1, 0), prim(-1))
            self.along(0, 0)
            self.along(0, 1)
            self.across(0, 0)

        def to(self, last):
            while self.done <= last:
                self.step(self.done)
                self.done += 1

        def step(self, n):
            i, j, h = key = ORDER[n]
            landed(self.shard(i, j, c, h), self.ss.at[n], self.rs.at[n])
            if key == (-1, 0, 0):
                self.send(key, (2, 0), prim(1))
            if key == (1, 0, 1):
                self.send(key, (2, 0), prim(-1))
            if j == 0:
                self.along(i, h)
            if j == -1 and h == 0:
                self.send(key, (i, 2), sec(1))
            if j == 1 and h == 1:
                self.send(key, (i, 2), sec(-1))
            if (i, j) in self.here:
                self.across(i, j)
            self.here.add((i, j))

        def sibling(self, i, j):
            k = len(ORDER) + SHARDS.index((i, j))
            landed(self.shard(i, j, 1 - c), self.ss.at[k], self.rs.at[k])

    gf = Gather(F, fs, fr, feature_sends)
    gt = Gather(T, ts, tr, pending)

    loads[0].wait()
    tw = text[...].astype(F32)
    T[own, :] = (tw * rms_scale(tw)).astype(BF)
    loads[1].wait()
    POS[g] = jnp.broadcast_to(pos[...].astype(F32), (8, ROWS))
    loads[2].wait()
    pl.semaphore_wait(barrier, len(partners))

    gf.start()
    mine = F.at[pl.ds(SLAB + g * ROWS, ROWS)]
    for k in (1, 3, 2):
        send(F.at[own], mine, zs.at[k - 1], zr.at[k - 1], zed(k), feature_sends)
        send(POS.at[g], POS.at[g], zs.at[k + 2], zr.at[k + 2], zed(k))
    gf.to(24)
    gt.start()
    gf.to(29)
    gt.to(3)
    for i, j in SHARDS:
        gf.sibling(i, j)

    def from_zed(k):
        return (g - k + 4) % 4

    for k in (1, 2, 3):
        o = from_zed(k)
        landed(F.at[pl.ds(SLAB + o * ROWS, ROWS)], zs.at[k - 1], zr.at[k - 1])

    for load in loads[3:]:
        load.wait()
    for r in range(2):
        rows = pl.ds(r * BLOCK, BLOCK)
        agg = jnp.zeros((BLOCK, D), F32)
        for k in range(K):
            b = cols[r, k]
            device = b // 2
            group, domain = device // N_DOM, device % N_DOM
            at = jnp.where(group == g, domain * 2 + b % 2, SLAB // BLOCK + group * 2 + b % 2)
            agg = agg + dot(adj[rows, k * BLOCK:(k + 1) * BLOCK], F[pl.ds(at * BLOCK, BLOCK), :])
        high = agg.astype(BF)
        rest = agg - high.astype(F32)
        low = rest.astype(BF)
        lowest = (rest - low.astype(F32)).astype(BF)
        AGG[pl.ds(c * ROWS + r * BLOCK, BLOCK), :] = high
        pre = (
            dot(F[pl.ds(d * ROWS + r * BLOCK, BLOCK), :], self_w[...])
            + (dot(high, nbr_w[...]) + (dot(low, nbr_w[...]) + dot(lowest, nbr_w[...])))
            + bias[...]
        )
        hidden = jnp.maximum(pre, 0.0)
        HID[rows, :] = hidden
        emb[rows, :] = hidden.astype(BF)
        Q[g, rows, :] = (hidden * rms_scale(hidden)).astype(BF)
        gt.to(5 + 2 * r)

    for k in (1, 3):
        send(Q.at[g], Q.at[g], zs.at[k + 5], zr.at[k + 5], zed(k))
    agg_own = AGG.at[pl.ds(c * ROWS, ROWS)]
    send(agg_own, agg_own, ms.at[0], mr.at[0], sib)
    emb_out = pltpu.make_async_copy(emb, emb_h, ls.at[8])
    emb_out.start()

    for k in (1, 2, 3):
        o = from_zed(k)
        landed(POS.at[o], zs.at[k + 2], zr.at[k + 2])
    lanes = lax.broadcasted_iota(jnp.int32, (ROWS, 128), 1).astype(F32)
    for o in range(N_GRP):
        PCOL[o] = column(POS[o, 0:1, :]) - lanes
    TACC[...] = jnp.zeros_like(TACC)
    PACC[...] = jnp.zeros_like(PACC)
    sib_rows = pl.ds((1 - c) * ROWS, ROWS)
    landed(AGG.at[sib_rows], ms.at[0], mr.at[0])
    pair = F[pl.ds((d // 2) * 2 * ROWS, 2 * ROWS), :]
    LT[...] = jnp.transpose(jnp.where(c == 0, pair, AGG[...]))
    drain(feature_sends)

    def doms_of(u, v):
        return [dom_at(i, j, c if v == 0 else 1 - c) for i, j in SHARDS[4 * u:4 * u + 4]]

    def offsets(dom):
        return [(g * SLAB + dom * ROWS + m * 128).astype(F32) for m in range(ROWS // 128)]

    def texts(u):
        doms = doms_of(u, 0) + doms_of(u, 1)
        ats = [at for dom in doms for at in offsets(dom)]
        return jnp.concatenate([T[pl.ds(dom * ROWS, ROWS), :] for dom in doms], axis=0), ats

    def exponentials(o, u):
        part, ats = texts(u)
        logits = dot_nt(Q[o], part)
        for r in range(0, ROWS, STRIP):
            rows = slice(r, r + STRIP)
            tot, picked, where = TACC[o, rows, :], PACC[o, rows, :], PCOL[o, rows, :]
            for m, at in enumerate(ats):
                tile = logits[rows, m * 128:(m + 1) * 128]
                e = jnp.exp2(tile * (SCALE * LOG2E))
                tot = tot + e
                picked = picked + jnp.where(where == at, tile, 0.0)
                lane = (m % 8) * 128
                base = (u * 2 + m // 8) * WIDE + o * ROWS + r
                FE[pl.ds(base, STRIP), lane:lane + 128] = e.astype(BF)
            TACC[o, rows, :] = tot
            PACC[o, rows, :] = picked

    def arrive(u):
        gt.to(UNITS[u])
        for i, j in SHARDS[4 * u:4 * u + 4]:
            gt.sibling(i, j)

    def queries(k):
        o = (g + k) % 4
        landed(Q.at[o], zs.at[9 - k], zr.at[9 - k])

    arrive(0)
    exponentials(g, 0)
    gt.to(11)
    arrive(1)
    send(Q.at[g], Q.at[g], zs.at[7], zr.at[7], zed(2))
    exponentials(g, 1)
    gt.to(17)
    for k, last in ((1, 19), (3, 23)):
        queries(k)
        for u in (0, 1):
            exponentials((g + k) % 4, u)
            gt.to(last + 2 * u if k == 1 else min(24, last + u))
    gt.to(24)
    arrive(2)
    for k in (0, 1, 3):
        exponentials((g + k) % 4, 2)
    queries(2)
    for u in range(3):
        exponentials((g + 2) % 4, u)
        gt.to((27, 29, 29)[u])
    arrive(3)
    for o in range(N_GRP):
        exponentials(o, 3)
    for o in range(N_GRP):
        TP_S[o] = jnp.concatenate(
            [lane_sums(TACC[o]), lane_sums(PACC[o]), jnp.zeros((6, ROWS), F32)], axis=0
        )
    for k in (2, 1, 3):
        send(TP_S, TP_R.at[k - 1], zs.at[8 + k], zr.at[8 + k], zed(k))

    index = lax.broadcasted_iota(jnp.int32, (ROWS, 128), 0) % 64
    factor = 1.0 + (2 * index + 1).astype(F32) * (1.0 / 128)

    def totals(o):
        return TP_S[o] + TP_R[0, o] + TP_R[1, o] + TP_R[2, o]

    for k in (1, 3, 2):
        landed(TP_R.at[k - 1], zs.at[8 + k], zr.at[8 + k])
    for o in range(N_GRP):
        RT[o] = factor / column(totals(o)[0:1, :])

    def weigh(o):
        acc = jnp.zeros((ROWS, H), F32)
        for u in range(4):
            part, ats = texts(u)
            strips = []
            for r in range(0, ROWS, STRIP):
                rows = slice(r, r + STRIP)
                inverse, where, unit = RT[o, rows, :], PCOL[o, rows, :], factor[rows, :]
                tiles = []
                for m, at in enumerate(ats):
                    lane = (m % 8) * 128
                    base = (u * 2 + m // 8) * WIDE + o * ROWS + r
                    e = FE[pl.ds(base, STRIP), lane:lane + 128]
                    w = e.astype(F32) * inverse
                    tiles.append((w - jnp.where(where == at, unit, 0.0)).astype(BF))
                strips.append(jnp.concatenate(tiles, axis=1))
            acc = acc + dot(jnp.concatenate(strips, axis=0), part)
        return acc

    for j in range(3):
        o = j + jnp.where(j < g, 0, 1)
        k = (o - g + 4) % 4
        W_S[j] = weigh(o).astype(BF)
        send(W_S.at[j], W_R.at[k - 1], zs.at[12 + j], zr.at[11 + k], (o, d))
    W_O[...] = weigh(g)

    for k in (1, 2, 3):
        landed(W_R.at[k - 1], zs.at[11 + k], zr.at[11 + k])

    unit = W_O[...]
    for k in range(3):
        unit = unit + W_R[k].astype(F32)
    unit = unit * (SCALE / factor[:, 0:1])
    sums = totals(g)
    loss = jnp.sum(jnp.log(sums[0:1, :]) - SCALE * sums[1:2, :], axis=1, keepdims=True)
    hidden = HID[...]
    scale_rows = rms_scale(hidden)
    normed = hidden * scale_rows
    back = scale_rows * (unit - normed * jnp.mean(unit * normed, axis=1, keepdims=True))
    grad_pre = jnp.where(hidden > 0, back, 0.0)
    G[pl.ds(c * ROWS, ROWS), :] = grad_pre.astype(BF)
    g_own = G.at[pl.ds(c * ROWS, ROWS)]
    send(g_own, g_own, ms.at[1], mr.at[1], sib)

    bias_sum = jnp.sum(grad_pre, axis=0, keepdims=True)
    parts = [bias_sum[:, m * 128:(m + 1) * 128] for m in range(4)]
    parts.append(jnp.broadcast_to(loss, (1, 128)))
    parts.append(jnp.zeros((3, 128), F32))
    extra = split(jnp.concatenate(parts, axis=0))

    landed(G.at[sib_rows], ms.at[1], mr.at[1])

    for k in (1, 3, 2, 0):
        m = (pi + k) % 4
        columns = pl.ds(pl.multiple_of(m * 128, 128), 128)
        SA[m, 0:D, :] = dot(LT[...], G[:, columns]).astype(BF)
        SA[m, D:D + 16, :] = extra
        if k:
            send(SA.at[m], RA.at[k - 1], gs.at[k - 1], gr.at[k - 1], prim(k))
    total = SA[pi].astype(F32)
    for k in (1, 3, 2):
        landed(RA.at[k - 1], gs.at[k - 1], gr.at[k - 1])
        total = total + RA[k - 1].astype(F32)
    extra = split(join(total[D:D + 16, :]))

    for m in range(16):
        SB[m, 0:48, :] = total[m * 48:(m + 1) * 48, :].astype(BF)
        SB[m, 48:64, :] = extra
    me = si * 4 + g
    for n, (j, k) in enumerate(across):
        m = ((si + j) % 4) * 4 + (g + k) % 4
        send(SB.at[m], RB.at[n], gs.at[3 + n], gr.at[3 + n], wall(j, k))
    total = SB[me].astype(F32)
    for n in range(15):
        landed(RB.at[n], gs.at[3 + n], gr.at[3 + n])
        total = total + RB[n].astype(F32)

    EX[c] = split(join(total[48:64, :]))
    send(EX.at[c], EX.at[c], ms.at[2], mr.at[2], sib)

    def piece(j, k):
        return GR.at[c, pl.ds(pi * 768 + ((si + j + 4) % 4) * 192 + ((g + k + 4) % 4) * 48, 48)]

    GR[c, pl.ds(pi * 768 + si * 192 + g * 48, 48), :] = total[0:48, :].astype(BF)
    for n, (j, k) in enumerate(across):
        send(piece(0, 0), piece(0, 0), gs.at[18 + n], gr.at[18 + n], wall(j, k))
    for n, (j, k) in enumerate(across):
        landed(piece(-j, -k), gs.at[18 + n], gr.at[18 + n])

    def block(k, cc):
        index = x * (1 - cc) + y * cc
        return ((index + k + 4) % 4) * 768

    def both(k, cc):
        return GR.at[cc, pl.ds(block(k, cc), 768)]

    outs = []

    def write(k, cc):
        at = pl.ds(block(k, cc), 768)
        cp = pltpu.make_async_copy(GR.at[cc, at], grads_h.at[cc, at], ls.at[9 + len(outs)])
        cp.start()
        outs.append(cp)

    for k in (1, 3, 2):
        send(both(0, c), both(0, c), gs.at[32 + k], gr.at[32 + k], prim(k))
    send(both(0, c), both(0, c), ms.at[3], mr.at[3], sib)
    write(0, c)
    landed(EX.at[1 - c], ms.at[2], mr.at[2])
    XO[...] = join(EX[0].astype(F32)) + join(EX[1].astype(F32))
    extra_out = pltpu.make_async_copy(XO, extra_h, ls.at[17])
    extra_out.start()
    for k in (1, 3, 2):
        landed(both(-k, c), gs.at[32 + k], gr.at[32 + k])
        send(both(-k, c), both(-k, c), ms.at[3 + k], mr.at[3 + k], sib)
        write(-k, c)
    for k in (0, 1, 3, 2):
        landed(both(-k, 1 - c), ms.at[3 + k], mr.at[3 + k])
        write(-k, 1 - c)
    for cp in outs:
        cp.wait()
    emb_out.wait()
    extra_out.wait()
    drain(pending)


def finish(emb_in, grads, extra, emb, loss, grad_self, grad_nbr, grad_bias):
    emb[...] = emb_in[...]
    loss[...] = extra[4:5, 0:1] * (1.0 / NODES)
    for m in range(4):
        at = slice(m * 128, (m + 1) * 128)
        grad_self[:, at] = grads[0, m * D:(m + 1) * D, :].astype(F32)
        grad_nbr[:, at] = grads[1, m * D:(m + 1) * D, :].astype(F32)
        grad_bias[:, at] = extra[m:m + 1, :]


def shards(features, text_embed, adjacency, block_cols, positive, self_weight, nbr_weight, hidden_bias):
    vmem = pl.BlockSpec(memory_space=pltpu.VMEM)
    hbm = pl.BlockSpec(memory_space=pl.ANY)
    dma = pltpu.SemaphoreType.DMA
    emb, grads, extra = pl.pallas_call(
        kernel,
        name="step",
        out_shape=(
            jax.ShapeDtypeStruct((ROWS, H), BF),
            jax.ShapeDtypeStruct((2, 4 * D, 128), BF),
            jax.ShapeDtypeStruct((8, 128), F32),
        ),
        in_specs=[hbm] * 8,
        out_specs=(hbm,) * 3,
        scratch_shapes=[
            pltpu.VMEM((SLAB + N_GRP * ROWS, WIDE), BF),
            pltpu.VMEM((SLAB, H), BF),
            pltpu.VMEM((N_GRP, ROWS, H), BF),
            pltpu.VMEM((N_GRP, 8, ROWS), F32),
            pltpu.VMEM((N_GRP, ROWS, 128), F32),
            pltpu.VMEM((2 * ROWS, D), BF),
            pltpu.VMEM((ROWS, H), F32),
            pltpu.VMEM((2 * ROWS, H), BF),
            pltpu.VMEM((D, 2 * ROWS), BF),
            pltpu.VMEM((N_GRP, ROWS, 128), F32),
            pltpu.VMEM((N_GRP, ROWS, 128), F32),
            pltpu.VMEM((N_GRP, ROWS, 128), F32),
            pltpu.VMEM((3, ROWS, H), BF),
            pltpu.VMEM((3, ROWS, H), BF),
            pltpu.VMEM((ROWS, H), F32),
            pltpu.VMEM((N_GRP, 8, ROWS), F32),
            pltpu.VMEM((3, N_GRP, 8, ROWS), F32),
            pltpu.VMEM((4, D + 16, 128), BF),
            pltpu.VMEM((3, D + 16, 128), BF),
            pltpu.VMEM((16, 64, 128), BF),
            pltpu.VMEM((15, 64, 128), BF),
            pltpu.VMEM((2, 16, 128), BF),
            pltpu.VMEM((2, 4 * D, 128), BF),
            pltpu.VMEM((8, 128), F32),
            pltpu.VMEM((ROWS, H), BF),
            pltpu.VMEM((ROWS, K * BLOCK), BF),
            pltpu.SMEM((2, K), jnp.int32),
            pltpu.VMEM((1, ROWS), jnp.int32),
            pltpu.VMEM((D, H), BF),
            pltpu.VMEM((D, H), BF),
            pltpu.VMEM((1, H), F32),
            pltpu.VMEM((ROWS, H), BF),
            dma((GATHER_SEMS,)), dma((GATHER_SEMS,)),
            dma((GATHER_SEMS,)), dma((GATHER_SEMS,)),
            dma((15,)), dma((15,)),
            dma((7,)), dma((7,)),
            dma((36,)), dma((36,)),
            dma((18,)),
        ],
        compiler_params=pltpu.CompilerParams(
            collective_id=0, has_side_effects=True, vmem_limit_bytes=56 * 2**20
        ),
        cost_estimate=pl.CostEstimate(
            flops=20 * 10**9, bytes_accessed=8 * 2**20, transcendentals=8 * 2**20
        ),
    )(
        features, text_embed, adjacency, block_cols, positive.reshape(1, ROWS), self_weight,
        nbr_weight, hidden_bias.reshape(1, H),
    )
    emb, loss, grad_self, grad_nbr, grad_bias = pl.pallas_call(
        finish,
        name="finish",
        out_shape=(
            jax.ShapeDtypeStruct((ROWS, H), BF),
            jax.ShapeDtypeStruct((1, 1), F32),
            jax.ShapeDtypeStruct((D, H), F32),
            jax.ShapeDtypeStruct((D, H), F32),
            jax.ShapeDtypeStruct((1, H), F32),
        ),
        in_specs=[vmem] * 3,
        out_specs=(vmem,) * 5,
    )(emb, grads, extra)
    return emb, loss.reshape(()), grad_self, grad_nbr, grad_bias.reshape(H)


def solution(mesh):
    rows = P(("grp", "dom"), None)
    return jax.shard_map(
        shards,
        mesh=mesh,
        in_specs=(rows, rows, rows, rows, P(("grp", "dom")), P(), P(), P()),
        out_specs=(rows, P(), P(), P(), P()),
        check_vma=False,
    )
```

```python
import jax
import jax.numpy as jnp
from jax import lax
from jax.experimental import pallas as pl
from jax.experimental.pallas import tpu as pltpu
from jax.sharding import PartitionSpec as P

MESH = pl.DeviceIdType.MESH
D = 768
H = 512
BLOCK = 128
K = 8
ROWS = 256
HALF = 128
N_GRP = 4
N_DOM = 32
NODES = 32768
SLAB = N_DOM * ROWS
WIDE = 1024
STRIP = 64

EPS = 1e-05
SCALE = 10.0 / H
LOG2E = 1.4426950408889634

BF = jnp.bfloat16
F32 = jnp.float32

ORDER = (
    (-1, 0, 0), (1, 0, 1), (-1, 0, 1), (1, 0, 0), (0, -1, 0), (0, 1, 0), (0, -1, 1), (0, 1, 1),
    (2, 0, 0), (-1, 1, 0), (-1, -1, 0), (2, 0, 1), (1, -1, 1), (1, 1, 1), (-1, -1, 1), (-1, 1, 1),
    (1, -1, 0), (1, 1, 0), (0, 2, 0), (0, 2, 1), (2, -1, 0), (2, 1, 0), (-1, 2, 0), (2, 1, 1),
    (2, -1, 1), (1, 2, 1), (-1, 2, 1), (1, 2, 0), (2, 2, 0), (2, 2, 1),
)
SHARDS = (
    (0, 0), (-1, 0), (1, 0), (0, -1), (0, 1), (2, 0), (-1, -1), (-1, 1),
    (1, -1), (1, 1), (0, 2), (2, -1), (2, 1), (-1, 2), (1, 2), (2, 2),
)
UNITS = (7, 15, 24, 29)
GATHER_SEMS = len(ORDER) + len(SHARDS)


def rms_scale(values):
    return lax.rsqrt(jnp.mean(values * values, axis=1, keepdims=True) + EPS)


def dot(a, b):
    return jnp.dot(a, b, preferred_element_type=F32)


def dot_nt(a, b):
    return lax.dot_general(a, b, (((1,), (1,)), ((), ())), preferred_element_type=F32)


def column(row):
    return jnp.transpose(jnp.broadcast_to(row, (128, ROWS)))


def lane_sums(a):
    return jnp.sum(jnp.transpose(a), axis=0, keepdims=True)


def split(v):
    high = v.astype(BF).astype(F32)
    return jnp.concatenate([high, v - high], axis=0).astype(BF)


def join(pair):
    return pair[0:8, :] + pair[8:16, :]


def kernel(
    feat_h, text_h, adj_h, cols_h, pos_h, self_h, nbr_h, bias_h,
    emb_h, grads_h, extra_h,
    FE, T, Q, POS, PCOL, AGG, HID, G, LT, TACC, PACC, RT, W_S, W_R, W_O, TP_S, TP_R,
    SA, RA, SB, RB, EX, GR, XO,
    text, adj, cols, pos, self_w, nbr_w, bias, emb,
    fs, fr, ts, tr, zs, zr, ms, mr, gs, gr, ls,
):
    g = lax.axis_index("grp")
    d = lax.axis_index("dom")
    c = d % 2
    x = (d // 2) % 4
    y = d // 8

    def dom_at(i, j, cc):
        ux, uy = 1 - cc, cc
        ax = (x + i * ux + j * uy + 4) % 4
        ay = (y + i * uy + j * ux + 4) % 4
        return (ay * 4 + ax) * 2 + cc

    def prim(k):
        return (g, dom_at(k, 0, c))

    def sec(k):
        return (g, dom_at(0, k, c))

    def zed(k):
        return ((g + k) % 4, d)

    def wall(j, k):
        return ((g + k) % 4, dom_at(0, j, c))

    sib = (g, d + 1 - 2 * c)
    pi = x * (1 - c) + y * c
    si = x * c + y * (1 - c)
    F = FE.at[:, pl.ds(0, D)]

    barrier = pltpu.get_barrier_semaphore()
    across = [(j, k) for j in range(4) for k in range(4) if j or k]
    partners = [sib] + [prim(k) for k in (1, 2, 3)] + [wall(j, k) for j, k in across]
    for dev in partners:
        pl.semaphore_signal(barrier, inc=1, device_id=dev, device_id_type=MESH)

    own = pl.ds(d * ROWS, ROWS)
    loads = [
        pltpu.make_async_copy(src, dst, ls.at[n])
        for n, (src, dst) in enumerate((
            (text_h, text), (pos_h, pos), (feat_h, F.at[own]), (cols_h, cols), (bias_h, bias),
            (adj_h, adj), (self_h, self_w), (nbr_h, nbr_w),
        ))
    ]
    for load in loads:
        load.start()

    pending = []
    feature_sends = []

    def rcopy(src, dst, ssem, rsem, dev):
        return pltpu.make_async_remote_copy(
            src_ref=src, dst_ref=dst, send_sem=ssem, recv_sem=rsem,
            device_id=dev, device_id_type=MESH,
        )

    def send(src, dst, ssem, rsem, dev, kept=pending):
        cp = rcopy(src, dst, ssem, rsem, dev)
        cp.start()
        kept.append(cp)

    def landed(region, ssem, rsem):
        rcopy(region, region, ssem, rsem, sib).wait_recv()

    def drain(kept):
        for cp in kept:
            cp.wait_send()

    class Gather:
        def __init__(self, tab, ssem, rsem, kept):
            self.tab, self.ss, self.rs, self.kept = tab, ssem, rsem, kept
            self.here = set()
            self.done = 0

        def shard(self, i, j, cc, half=None):
            base = dom_at(i, j, cc) * ROWS
            if half is None:
                return self.tab.at[pl.ds(base, ROWS)]
            return self.tab.at[pl.ds(base + half * HALF, HALF)]

        def send(self, key, to, dev):
            ref = self.shard(key[0], key[1], c, key[2])
            k = ORDER.index(to + (key[2],))
            send(ref, ref, self.ss.at[k], self.rs.at[k], dev, self.kept)

        def across(self, i, j):
            ref = self.shard(i, j, c)
            k = len(ORDER) + SHARDS.index((i, j))
            send(ref, ref, self.ss.at[k], self.rs.at[k], sib, self.kept)

        def along(self, i, h):
            self.send((i, 0, h), (i, -1), sec(1))
            self.send((i, 0, h), (i, 1), sec(-1))

        def start(self):
            self.send((0, 0, 0), (-1, 0), prim(1))
            self.send((0, 0, 1), (1, 0), prim(-1))
            self.send((0, 0, 1), (-1, 0), prim(1))
            self.send((0, 0, 0), (1, 0), prim(-1))
            self.along(0, 0)
            self.along(0, 1)
            self.across(0, 0)

        def to(self, last):
            while self.done <= last:
                self.step(self.done)
                self.done += 1

        def step(self, n):
            i, j, h = key = ORDER[n]
            landed(self.shard(i, j, c, h), self.ss.at[n], self.rs.at[n])
            if key == (-1, 0, 0):
                self.send(key, (2, 0), prim(1))
            if key == (1, 0, 1):
                self.send(key, (2, 0), prim(-1))
            if j == 0:
                self.along(i, h)
            if j == -1 and h == 0:
                self.send(key, (i, 2), sec(1))
            if j == 1 and h == 1:
                self.send(key, (i, 2), sec(-1))
            if (i, j) in self.here:
                self.across(i, j)
            self.here.add((i, j))

        def sibling(self, i, j):
            k = len(ORDER) + SHARDS.index((i, j))
            landed(self.shard(i, j, 1 - c), self.ss.at[k], self.rs.at[k])

    gf = Gather(F, fs, fr, feature_sends)
    gt = Gather(T, ts, tr, pending)

    loads[0].wait()
    tw = text[...].astype(F32)
    T[own, :] = (tw * rms_scale(tw)).astype(BF)
    loads[1].wait()
    POS[g] = jnp.broadcast_to(pos[...].astype(F32), (8, ROWS))
    loads[2].wait()
    pl.semaphore_wait(barrier, len(partners))

    gf.start()
    mine = F.at[pl.ds(SLAB + g * ROWS, ROWS)]
    for k in (1, 3, 2):
        send(F.at[own], mine, zs.at[k - 1], zr.at[k - 1], zed(k), feature_sends)
        send(POS.at[g], POS.at[g], zs.at[k + 2], zr.at[k + 2], zed(k))
    gf.to(24)
    gt.start()
    gf.to(29)
    gt.to(3)
    for i, j in SHARDS:
        gf.sibling(i, j)

    def from_zed(k):
        return (g - k + 4) % 4

    for k in (1, 2, 3):
        o = from_zed(k)
        landed(F.at[pl.ds(SLAB + o * ROWS, ROWS)], zs.at[k - 1], zr.at[k - 1])

    for load in loads[3:]:
        load.wait()
    for r in range(2):
        rows = pl.ds(r * BLOCK, BLOCK)
        agg = jnp.zeros((BLOCK, D), F32)
        for k in range(K):
            b = cols[r, k]
            device = b // 2
            group, domain = device // N_DOM, device % N_DOM
            at = jnp.where(group == g, domain * 2 + b % 2, SLAB // BLOCK + group * 2 + b % 2)
            agg = agg + dot(adj[rows, k * BLOCK:(k + 1) * BLOCK], F[pl.ds(at * BLOCK, BLOCK), :])
        high = agg.astype(BF)
        rest = agg - high.astype(F32)
        low = rest.astype(BF)
        lowest = (rest - low.astype(F32)).astype(BF)
        AGG[pl.ds(c * ROWS + r * BLOCK, BLOCK), :] = high
        pre = (
            dot(F[pl.ds(d * ROWS + r * BLOCK, BLOCK), :], self_w[...])
            + (dot(high, nbr_w[...]) + (dot(low, nbr_w[...]) + dot(lowest, nbr_w[...])))
            + bias[...]
        )
        hidden = jnp.maximum(pre, 0.0)
        HID[rows, :] = hidden
        emb[rows, :] = hidden.astype(BF)
        Q[g, rows, :] = (hidden * rms_scale(hidden)).astype(BF)
        gt.to(5 + 2 * r)

    for k in (1, 3):
        send(Q.at[g], Q.at[g], zs.at[k + 5], zr.at[k + 5], zed(k))
    agg_own = AGG.at[pl.ds(c * ROWS, ROWS)]
    send(agg_own, agg_own, ms.at[0], mr.at[0], sib)
    emb_out = pltpu.make_async_copy(emb, emb_h, ls.at[8])
    emb_out.start()

    for k in (1, 2, 3):
        o = from_zed(k)
        landed(POS.at[o], zs.at[k + 2], zr.at[k + 2])
    lanes = lax.broadcasted_iota(jnp.int32, (ROWS, 128), 1).astype(F32)
    for o in range(N_GRP):
        PCOL[o] = column(POS[o, 0:1, :]) - lanes
    TACC[...] = jnp.zeros_like(TACC)
    PACC[...] = jnp.zeros_like(PACC)
    sib_rows = pl.ds((1 - c) * ROWS, ROWS)
    landed(AGG.at[sib_rows], ms.at[0], mr.at[0])
    pair = F[pl.ds((d // 2) * 2 * ROWS, 2 * ROWS), :]
    LT[...] = jnp.transpose(jnp.where(c == 0, pair, AGG[...]))
    drain(feature_sends)

    def doms_of(u, v):
        return [dom_at(i, j, c if v == 0 else 1 - c) for i, j in SHARDS[4 * u:4 * u + 4]]

    def offsets(dom):
        return [(g * SLAB + dom * ROWS + m * 128).astype(F32) for m in range(ROWS // 128)]

    def texts(u):
        doms = doms_of(u, 0) + doms_of(u, 1)
        ats = [at for dom in doms for at in offsets(dom)]
        return jnp.concatenate([T[pl.ds(dom * ROWS, ROWS), :] for dom in doms], axis=0), ats

    def exponentials(o, u):
        part, ats = texts(u)
        logits = dot_nt(Q[o], part)
        for r in range(0, ROWS, STRIP):
            rows = slice(r, r + STRIP)
            tot, picked, where = TACC[o, rows, :], PACC[o, rows, :], PCOL[o, rows, :]
            for m, at in enumerate(ats):
                tile = logits[rows, m * 128:(m + 1) * 128]
                e = jnp.exp2(tile * (SCALE * LOG2E))
                tot = tot + e
                picked = picked + jnp.where(where == at, tile, 0.0)
                lane = (m % 8) * 128
                base = (u * 2 + m // 8) * WIDE + o * ROWS + r
                FE[pl.ds(base, STRIP), lane:lane + 128] = e.astype(BF)
            TACC[o, rows, :] = tot
            PACC[o, rows, :] = picked

    def arrive(u):
        gt.to(UNITS[u])
        for i, j in SHARDS[4 * u:4 * u + 4]:
            gt.sibling(i, j)

    def queries(k):
        o = (g + k) % 4
        landed(Q.at[o], zs.at[9 - k], zr.at[9 - k])

    arrive(0)
    exponentials(g, 0)
    gt.to(11)
    arrive(1)
    send(Q.at[g], Q.at[g], zs.at[7], zr.at[7], zed(2))
    exponentials(g, 1)
    gt.to(17)
    for k, last in ((1, 19), (3, 23)):
        queries(k)
        for u in (0, 1):
            exponentials((g + k) % 4, u)
            gt.to(last + 2 * u if k == 1 else min(24, last + u))
    gt.to(24)
    arrive(2)
    for k in (0, 1, 3):
        exponentials((g + k) % 4, 2)
    queries(2)
    for u in range(3):
        exponentials((g + 2) % 4, u)
        gt.to((27, 29, 29)[u])
    arrive(3)
    for o in range(N_GRP):
        exponentials(o, 3)
    for o in range(N_GRP):
        TP_S[o] = jnp.concatenate(
            [lane_sums(TACC[o]), lane_sums(PACC[o]), jnp.zeros((6, ROWS), F32)], axis=0
        )
    for k in (2, 1, 3):
        send(TP_S, TP_R.at[k - 1], zs.at[8 + k], zr.at[8 + k], zed(k))

    index = lax.broadcasted_iota(jnp.int32, (ROWS, 128), 0) % 64
    factor = 1.0 + (2 * index + 1).astype(F32) * (1.0 / 128)

    def totals(o):
        return TP_S[o] + TP_R[0, o] + TP_R[1, o] + TP_R[2, o]

    for k in (1, 3, 2):
        landed(TP_R.at[k - 1], zs.at[8 + k], zr.at[8 + k])
    for o in range(N_GRP):
        RT[o] = factor / column(totals(o)[0:1, :])

    def weigh(o):
        acc = jnp.zeros((ROWS, H), F32)
        for u in range(4):
            part, ats = texts(u)
            strips = []
            for r in range(0, ROWS, STRIP):
                rows = slice(r, r + STRIP)
                inverse, where, unit = RT[o, rows, :], PCOL[o, rows, :], factor[rows, :]
                tiles = []
                for m, at in enumerate(ats):
                    lane = (m % 8) * 128
                    base = (u * 2 + m // 8) * WIDE + o * ROWS + r
                    e = FE[pl.ds(base, STRIP), lane:lane + 128]
                    w = e.astype(F32) * inverse
                    tiles.append((w - jnp.where(where == at, unit, 0.0)).astype(BF))
                strips.append(jnp.concatenate(tiles, axis=1))
            acc = acc + dot(jnp.concatenate(strips, axis=0), part)
        return acc

    for j in range(3):
        o = j + jnp.where(j < g, 0, 1)
        k = (o - g + 4) % 4
        W_S[j] = weigh(o).astype(BF)
        send(W_S.at[j], W_R.at[k - 1], zs.at[12 + j], zr.at[11 + k], (o, d))
    W_O[...] = weigh(g)

    for k in (1, 2, 3):
        landed(W_R.at[k - 1], zs.at[11 + k], zr.at[11 + k])

    unit = W_O[...]
    for k in range(3):
        unit = unit + W_R[k].astype(F32)
    unit = unit * (SCALE / factor[:, 0:1])
    sums = totals(g)
    loss = jnp.sum(jnp.log(sums[0:1, :]) - SCALE * sums[1:2, :], axis=1, keepdims=True)
    hidden = HID[...]
    scale_rows = rms_scale(hidden)
    normed = hidden * scale_rows
    back = scale_rows * (unit - normed * jnp.mean(unit * normed, axis=1, keepdims=True))
    grad_pre = jnp.where(hidden > 0, back, 0.0)
    G[pl.ds(c * ROWS, ROWS), :] = grad_pre.astype(BF)
    g_own = G.at[pl.ds(c * ROWS, ROWS)]
    send(g_own, g_own, ms.at[1], mr.at[1], sib)

    bias_sum = jnp.sum(grad_pre, axis=0, keepdims=True)
    parts = [bias_sum[:, m * 128:(m + 1) * 128] for m in range(4)]
    parts.append(jnp.broadcast_to(loss, (1, 128)))
    parts.append(jnp.zeros((3, 128), F32))
    extra = split(jnp.concatenate(parts, axis=0))

    landed(G.at[sib_rows], ms.at[1], mr.at[1])

    for k in (1, 3, 2, 0):
        m = (pi + k) % 4
        columns = pl.ds(pl.multiple_of(m * 128, 128), 128)
        SA[m, 0:D, :] = dot(LT[...], G[:, columns]).astype(BF)
        SA[m, D:D + 16, :] = extra
        if k:
            send(SA.at[m], RA.at[k - 1], gs.at[k - 1], gr.at[k - 1], prim(k))
    total = SA[pi].astype(F32)
    for k in (1, 3, 2):
        landed(RA.at[k - 1], gs.at[k - 1], gr.at[k - 1])
        total = total + RA[k - 1].astype(F32)
    extra = split(join(total[D:D + 16, :]))

    for m in range(16):
        SB[m, 0:48, :] = total[m * 48:(m + 1) * 48, :].astype(BF)
        SB[m, 48:64, :] = extra
    me = si * 4 + g
    for n, (j, k) in enumerate(across):
        m = ((si + j) % 4) * 4 + (g + k) % 4
        send(SB.at[m], RB.at[n], gs.at[3 + n], gr.at[3 + n], wall(j, k))
    total = SB[me].astype(F32)
    for n in range(15):
        landed(RB.at[n], gs.at[3 + n], gr.at[3 + n])
        total = total + RB[n].astype(F32)

    EX[c] = split(join(total[48:64, :]))
    send(EX.at[c], EX.at[c], ms.at[2], mr.at[2], sib)

    def piece(j, k):
        return GR.at[c, pl.ds(pi * 768 + ((si + j + 4) % 4) * 192 + ((g + k + 4) % 4) * 48, 48)]

    GR[c, pl.ds(pi * 768 + si * 192 + g * 48, 48), :] = total[0:48, :].astype(BF)
    for n, (j, k) in enumerate(across):
        send(piece(0, 0), piece(0, 0), gs.at[18 + n], gr.at[18 + n], wall(j, k))
    for n, (j, k) in enumerate(across):
        landed(piece(-j, -k), gs.at[18 + n], gr.at[18 + n])

    def block(k, cc):
        index = x * (1 - cc) + y * cc
        return ((index + k + 4) % 4) * 768

    def both(k, cc):
        return GR.at[cc, pl.ds(block(k, cc), 768)]

    outs = []

    def write(k, cc):
        at = pl.ds(block(k, cc), 768)
        cp = pltpu.make_async_copy(GR.at[cc, at], grads_h.at[cc, at], ls.at[9 + len(outs)])
        cp.start()
        outs.append(cp)

    for k in (1, 3, 2):
        send(both(0, c), both(0, c), gs.at[32 + k], gr.at[32 + k], prim(k))
    send(both(0, c), both(0, c), ms.at[3], mr.at[3], sib)
    write(0, c)
    landed(EX.at[1 - c], ms.at[2], mr.at[2])
    XO[...] = join(EX[0].astype(F32)) + join(EX[1].astype(F32))
    extra_out = pltpu.make_async_copy(XO, extra_h, ls.at[17])
    extra_out.start()
    for k in (1, 3, 2):
        landed(both(-k, c), gs.at[32 + k], gr.at[32 + k])
        send(both(-k, c), both(-k, c), ms.at[3 + k], mr.at[3 + k], sib)
        write(-k, c)
    for k in (0, 1, 3, 2):
        landed(both(-k, 1 - c), ms.at[3 + k], mr.at[3 + k])
        write(-k, 1 - c)
    for cp in outs:
        cp.wait()
    emb_out.wait()
    extra_out.wait()
    drain(pending)


def finish(emb_in, grads, extra, emb, loss, grad_self, grad_nbr, grad_bias):
    emb[...] = emb_in[...]
    loss[...] = extra[4:5, 0:1] * (1.0 / NODES)
    for m in range(4):
        at = slice(m * 128, (m + 1) * 128)
        grad_self[:, at] = grads[0, m].astype(F32)
        grad_nbr[:, at] = grads[1, m].astype(F32)
        grad_bias[:, at] = extra[m:m + 1, :]


def shards(features, text_embed, adjacency, block_cols, positive, self_weight, nbr_weight, hidden_bias):
    hbm = pl.BlockSpec(memory_space=pl.ANY)
    dma = pltpu.SemaphoreType.DMA
    emb, grads, extra = pl.pallas_call(
        kernel,
        name="step",
        out_shape=(
            jax.ShapeDtypeStruct((ROWS, H), BF),
            jax.ShapeDtypeStruct((2, 4 * D, 128), BF),
            jax.ShapeDtypeStruct((8, 128), F32),
        ),
        in_specs=[hbm] * 8,
        out_specs=(hbm,) * 3,
        scratch_shapes=[
            pltpu.VMEM((SLAB + N_GRP * ROWS, WIDE), BF),
            pltpu.VMEM((SLAB, H), BF),
            pltpu.VMEM((N_GRP, ROWS, H), BF),
            pltpu.VMEM((N_GRP, 8, ROWS), F32),
            pltpu.VMEM((N_GRP, ROWS, 128), F32),
            pltpu.VMEM((2 * ROWS, D), BF),
            pltpu.VMEM((ROWS, H), F32),
            pltpu.VMEM((2 * ROWS, H), BF),
            pltpu.VMEM((D, 2 * ROWS), BF),
            pltpu.VMEM((N_GRP, ROWS, 128), F32),
            pltpu.VMEM((N_GRP, ROWS, 128), F32),
            pltpu.VMEM((N_GRP, ROWS, 128), F32),
            pltpu.VMEM((3, ROWS, H), BF),
            pltpu.VMEM((3, ROWS, H), BF),
            pltpu.VMEM((ROWS, H), F32),
            pltpu.VMEM((N_GRP, 8, ROWS), F32),
            pltpu.VMEM((3, N_GRP, 8, ROWS), F32),
            pltpu.VMEM((4, D + 16, 128), BF),
            pltpu.VMEM((3, D + 16, 128), BF),
            pltpu.VMEM((16, 64, 128), BF),
            pltpu.VMEM((15, 64, 128), BF),
            pltpu.VMEM((2, 16, 128), BF),
            pltpu.VMEM((2, 4 * D, 128), BF),
            pltpu.VMEM((8, 128), F32),
            pltpu.VMEM((ROWS, H), BF),
            pltpu.VMEM((ROWS, K * BLOCK), BF),
            pltpu.SMEM((2, K), jnp.int32),
            pltpu.VMEM((1, ROWS), jnp.int32),
            pltpu.VMEM((D, H), BF),
            pltpu.VMEM((D, H), BF),
            pltpu.VMEM((1, H), F32),
            pltpu.VMEM((ROWS, H), BF),
            dma((GATHER_SEMS,)), dma((GATHER_SEMS,)),
            dma((GATHER_SEMS,)), dma((GATHER_SEMS,)),
            dma((15,)), dma((15,)),
            dma((7,)), dma((7,)),
            dma((36,)), dma((36,)),
            dma((18,)),
        ],
        compiler_params=pltpu.CompilerParams(
            collective_id=0, has_side_effects=True, vmem_limit_bytes=56 * 2**20
        ),
        cost_estimate=pl.CostEstimate(
            flops=20 * 10**9, bytes_accessed=8 * 2**20, transcendentals=8 * 2**20
        ),
    )(
        features, text_embed, adjacency, block_cols, positive.reshape(1, ROWS), self_weight,
        nbr_weight, hidden_bias.reshape(1, H),
    )
    emb, loss, grad_self, grad_nbr, grad_bias = pl.pallas_call(
        finish,
        name="finish",
        out_shape=(
            jax.ShapeDtypeStruct((ROWS, H), BF),
            jax.ShapeDtypeStruct((1, 1), F32),
            jax.ShapeDtypeStruct((D, H), F32),
            jax.ShapeDtypeStruct((D, H), F32),
            jax.ShapeDtypeStruct((1, H), F32),
        ),
        grid=(4,),
        in_specs=[
            pl.BlockSpec((ROWS // 4, H), lambda i: (i, 0)),
            pl.BlockSpec((2, 4, D // 4, 128), lambda i: (0, 0, i, 0)),
            pl.BlockSpec((8, 128), lambda i: (0, 0)),
        ],
        out_specs=(
            pl.BlockSpec((ROWS // 4, H), lambda i: (i, 0)),
            pl.BlockSpec((1, 1), lambda i: (0, 0)),
            pl.BlockSpec((D // 4, H), lambda i: (i, 0)),
            pl.BlockSpec((D // 4, H), lambda i: (i, 0)),
            pl.BlockSpec((1, H), lambda i: (0, 0)),
        ),
    )(emb, grads.reshape(2, 4, D, 128), extra)
    return emb, loss.reshape(()), grad_self, grad_nbr, grad_bias.reshape(H)


def solution(mesh):
    rows = P(("grp", "dom"), None)
    return jax.shard_map(
        shards,
        mesh=mesh,
        in_specs=(rows, rows, rows, rows, P(("grp", "dom")), P(), P(), P()),
        out_specs=(rows, P(), P(), P(), P()),
        check_vma=False,
    )
```
